256 devices in a mesh: blk: 64 (over x, z, core), kv: 4 (over y).
Axes of the slice: x: 4, y: 4, z: 8, core: 2. Of those that a mesh axis runs over, the one named last changes fastest.
Arguments:
- queries: bfloat16 [8192, 128, 128], P(('blk', 'kv')), may hold values from -30 to 30
- cache_keys: bfloat16 [131072, 8, 128], P('blk', 'kv'), may hold values from -6 to 6
- cache_values: bfloat16 [131072, 8, 128], P('blk', 'kv'), may hold values from -48 to 48
- new_keys: bfloat16 [8192, 8, 128], P(('blk', 'kv')), may hold values from -6 to 6
- new_values: bfloat16 [8192, 8, 128], P(('blk', 'kv')), may hold values from -48 to 48
- counts: int32 [64], P('blk'), may hold values from 129 to 2048, as said below
Outputs:
- attended: bfloat16 [8192, 128, 128], P(('blk', 'kv'))
- logsum: float32 [8192, 128], P(('blk', 'kv'))
The draws below stay inside these ranges and needn't reach their ends.
Inputs may be any that keep to these rules, and one draw needn't show every extreme that they name: Segment b's live rows are its first counts[b] rows; some segment has all 2048 live.
All inputs are finite; a program needn't handle non-finite values.
Results may differ from the reference program's by a relative error of at most 0.015.
Values may be sent and summed in bfloat16 or wider, within the bound.
A program may use at most 64 MiB of HBM per device.

```python
import math
import jax
import jax.numpy as jnp
from jax import lax

QH = 128
KVH = 8
HD = 128
Q_DEV = 128
CAP = 2048
SPAN = 3
TURN = 8192
CACHE = 131072


def draw_queries(key, part):
    key = jax.random.fold_in(key, 1)
    entries = jnp.clip(jax.random.normal(key, (TURN, QH, HD), jnp.float32), -4.0, 4.0)
    return entries.astype(jnp.bfloat16)


def draw_cache_keys(key, part):
    key = jax.random.fold_in(key, 2)
    entries = jnp.clip(jax.random.normal(key, (CACHE, KVH, HD), jnp.float32), -4.0, 4.0)
    return entries.astype(jnp.bfloat16)


def draw_counts(key, part):
    key = jax.random.fold_in(key, 11)
    key_level, key_cut, key_full = jax.random.split(key, 3)
    segments = CACHE // CAP
    level = jax.random.randint(key_level, (segments,), 0, 4)
    base = CAP // jnp.left_shift(1, level)
    shaved = jax.random.randint(key_cut, (segments,), 0, CAP // 16)
    filled = jax.random.randint(key_full, (), 0, segments)
    result = jnp.where(jnp.arange(segments) == filled, CAP, base - shaved)
    return result.astype(jnp.int32)


def levels(rng, shape, cuts, smallest, largest):
    def one(position, parts):
        steps = jax.random.uniform(jax.random.fold_in(jax.random.fold_in(rng, 6), position), (parts,), jnp.float32, smallest / len(cuts), largest / len(cuts))
        return jnp.repeat(jnp.exp(steps), shape[position] // parts).reshape((-1,) + (1,) * (len(shape) - position - 1))

    level = one(*cuts[0])
    for cut in cuts[1:]:
        level = level * one(*cut)
    return level


def normal_values(rng, shape, width, limit, cuts=(), kind=jnp.bfloat16):
    gain = levels(rng, shape, cuts, -0.22, 0.18) if cuts else 1.0
    array = jax.random.normal(rng, shape, jnp.float32) * width * gain
    return jnp.minimum(jnp.maximum(array, -limit), limit).astype(kind)


def setup_inputs(seed: int = 0) -> dict:
    key_of = jax.random.split(jax.random.key(seed), 7)
    return {
        "queries": draw_queries(jax.random.fold_in(key_of[6], 71), 0),
        "cache_keys": draw_cache_keys(jax.random.fold_in(key_of[6], 71), 0),
        "cache_values": normal_values(key_of[2], (CACHE, KVH, HD), 8.0, 48.0, ((0, 64), (1, 4))),
        "new_keys": normal_values(key_of[3], (TURN, KVH, HD), 1.0, 6.0, ((0, 256),)),
        "new_values": normal_values(key_of[4], (TURN, KVH, HD), 8.0, 48.0, ((0, 256),)),
        "counts": draw_counts(jax.random.fold_in(key_of[6], 71), 0),
    }


MASKED = -1e+30

def reference(queries, cache_keys, cache_values, new_keys, new_values, counts):
    group_size = QH // KVH
    score_scale = 1.0 / math.sqrt(HD)
    segments = CACHE // CAP
    query_tiles = queries.reshape(segments, Q_DEV, KVH, group_size, HD)
    seg_keys = cache_keys.reshape(segments, CAP, KVH, HD)
    seg_values = cache_values.reshape(segments, CAP, KVH, HD)
    tile_keys = new_keys.reshape(segments, Q_DEV, KVH, HD)
    tile_values = new_values.reshape(segments, Q_DEV, KVH, HD)
    slot_index = jnp.arange(CAP, dtype=jnp.int32)
    token_index = jnp.arange(Q_DEV, dtype=jnp.int32)
    causal = jnp.where(token_index[None, :] <= token_index[:, None], 0.0, MASKED).astype(jnp.float32)

    def per_tile(tile_index):
        sources = ((tile_index - jnp.arange(SPAN, dtype=jnp.int32)) % segments).astype(jnp.int32)
        cache_rows = seg_keys[sources].reshape(SPAN * CAP, KVH, HD)
        cache_vals = seg_values[sources].reshape(SPAN * CAP, KVH, HD)
        usable = (slot_index[None, :] < counts[sources][:, None]).reshape(SPAN * CAP)
        cache_bias = jnp.where(usable, 0.0, MASKED).astype(jnp.float32)
        all_bias = jnp.concatenate([jnp.broadcast_to(cache_bias[None, :], (Q_DEV, SPAN * CAP)), causal], axis=1)
        all_keys = jnp.concatenate([cache_rows, tile_keys[tile_index]], axis=0).astype(jnp.float32)
        all_values = jnp.concatenate([cache_vals, tile_values[tile_index]], axis=0).astype(jnp.float32)
        query_block = query_tiles[tile_index].astype(jnp.float32)
        scores = jnp.einsum('qghd,kgd->qghk', query_block, all_keys) * score_scale
        scores = scores + all_bias[:, None, None, :]
        highest = lax.optimization_barrier(jnp.max(scores, axis=-1))
        weights = jnp.exp(scores - highest[..., None])
        totals = lax.optimization_barrier(jnp.sum(weights, axis=-1))
        weights_low = lax.optimization_barrier(weights.astype(jnp.bfloat16)).astype(jnp.float32)
        mixed = jnp.einsum('qghk,kgd->qghd', weights_low, all_values)
        output = (mixed / totals[..., None]).astype(jnp.bfloat16).reshape(Q_DEV, QH, HD)
        log_total = (highest + jnp.log(totals)).reshape(Q_DEV, QH)
        return (output, log_total)
    outputs, log_totals = lax.map(per_tile, jnp.arange(segments, dtype=jnp.int32))
    return (outputs.reshape(TURN, QH, HD), log_totals.reshape(TURN, QH))
```

```python
import functools
import math

import jax
import jax.numpy as jnp
from jax import lax
from jax.experimental import pallas as pl
from jax.experimental.pallas import tpu as pltpu
from jax.sharding import PartitionSpec as P

MESH = pl.DeviceIdType.MESH
LOG2E = math.log2(math.e)
NEG = -1e30
KC = 256
EXT = 16

ORDER = (
    ("X", 0), ("Z", 0), ("Y", 1), ("X", 1), ("Z", 1), ("X", 3),
    ("Z", 3), ("X", 2), ("Z", 2), ("Y", 3), ("Y", 2), ("Y", 0),
)
FINISH = {3: [(0, 0)], 5: [(1, 1)], 6: [(0, 1)], 8: [(0, 3)], 9: [(1, 3)], 10: [(0, 2), (1, 2)], 11: [(1, 0)]}
FORWARD = {0: [], 1: [1, 3], 5: [2]}


def look(position, values):
    result = jnp.int32(values[-1])
    for i in reversed(range(len(values) - 1)):
        result = jnp.where(position == i, jnp.int32(values[i]), result)
    return result


def dot(a, b, ca, cb):
    return lax.dot_general(a, b, (((ca,), (cb,)), ((), ())), preferred_element_type=jnp.float32)


def pack_log(value):
    hi = value.astype(jnp.bfloat16).astype(jnp.float32)
    mid = (value - hi).astype(jnp.bfloat16).astype(jnp.float32)
    low = value - hi - mid
    row = lax.broadcasted_iota(jnp.int32, (EXT, value.shape[1]), 0)
    packed = jnp.where(row == 0, hi, jnp.where(row == 1, mid, jnp.where(row == 2, low, 0.0)))
    return packed.astype(jnp.bfloat16)


def unpack_log(rows):
    wide = rows.astype(jnp.float32)
    return wide[0:1] + wide[1:2] + wide[2:3]


def kernel(
    nb, ny,
    counts, q_in, ck_in, cv_in, nk_in, nv_in,
    o_out, lse_out,
    raw_k, raw_v, wide, k_buf, v_buf, k_send, v_send, qall, new_raw, new_send, new_buf,
    s0, s1, m0, m1, p0, p1, acc_a, acc_b, res, part_in, o_stage, lse_stage,
    load_sem, q_send, q_recv, z_send, f_send, n_send, n_recv, x_send, x_recv,
    r_send, r_recv, o_send, o_recv, l_send, l_recv,
):
    cap = k_buf.shape[1]
    tok, grp, hd = qall.shape[1:]
    rows = tok * grp
    half = rows // 2
    scale = LOG2E / math.sqrt(hd)

    b = lax.axis_index("blk")
    y = lax.axis_index("kv")
    g = lax.rem(b, 2)
    chip0 = b - g
    prev0 = lax.rem(chip0 + nb - 2, nb)
    next0 = lax.rem(chip0 + 2, nb)
    other = (chip0 + 1 - g, y)

    def peer(dj, di):
        return lax.rem(g + di, 2), lax.rem(y + dj, ny)

    peers = [(dj, di) for dj in range(ny) for di in range(2) if (dj, di) != (0, 0)]

    load_k = pltpu.make_async_copy(ck_in, raw_k, load_sem.at[0])
    load_v = pltpu.make_async_copy(cv_in, raw_v, load_sem.at[1])
    load_nk = pltpu.make_async_copy(nk_in, new_raw.at[0], load_sem.at[2])
    load_nv = pltpu.make_async_copy(nv_in, new_raw.at[1], load_sem.at[3])
    load_k.start()
    load_nk.start()
    load_nv.start()
    load_v.start()

    def heads_of(gg, yy):
        return pl.ds(pl.multiple_of((2 * yy + gg) * grp, grp), grp)

    load_q = pltpu.make_async_copy(q_in.at[:, heads_of(g, y), :], qall.at[g], q_recv.at[g])
    load_q.start()

    barrier = pltpu.get_barrier_semaphore()
    for dj, di in peers:
        gg, yy = peer(dj, di)
        pl.semaphore_signal(barrier, inc=1, device_id=(chip0 + gg, yy), device_id_type=MESH)
    for base in (prev0, next0):
        for i in range(2):
            pl.semaphore_signal(barrier, inc=1, device_id=(base + i, y), device_id_type=MESH)
    pl.semaphore_wait(barrier, len(peers) + 4)

    def q_copy(n, dj, di):
        gg, yy = peer(dj, di)
        slot = ((ny - dj) % ny) * 2 + g
        return pltpu.make_async_remote_copy(
            src_ref=q_in.at[:, heads_of(gg, yy), :], dst_ref=qall.at[slot],
            send_sem=q_send.at[n], recv_sem=q_recv.at[slot],
            device_id=(chip0 + gg, yy), device_id_type=MESH,
        )

    def z_copy(gg):
        slot = 2 * ny + g
        return pltpu.make_async_remote_copy(
            src_ref=q_in.at[:, heads_of(gg, y), :], dst_ref=qall.at[slot],
            send_sem=z_send.at[gg], recv_sem=q_recv.at[slot],
            device_id=(prev0 + gg, y), device_id_type=MESH,
        )

    def forward_copy(slot):
        return pltpu.make_async_remote_copy(
            src_ref=qall.at[slot], dst_ref=qall.at[2 * ny + slot],
            send_sem=f_send.at[slot], recv_sem=q_recv.at[2 * ny + slot],
            device_id=(prev0 + g, y), device_id_type=MESH,
        )

    def q_wait(slot):
        pltpu.make_async_remote_copy(
            src_ref=qall.at[slot], dst_ref=qall.at[slot],
            send_sem=f_send.at[0], recv_sem=q_recv.at[slot],
            device_id=other, device_id_type=MESH,
        ).wait_recv()

    order = {}
    for n, pair in enumerate(peers):
        order[pair] = n
    send_order = sorted(peers, key=lambda pair: (0, ny - 1, 1, 2)[pair[0]] if ny == 4 else pair[0])
    send_order = [(0, 1)] + [pair for pair in send_order if pair != (0, 1)]
    q_copy(order[(0, 1)], 0, 1).start()
    z_copy(0).start()
    z_copy(1).start()
    for pair in send_order[1:]:
        q_copy(order[pair], *pair).start()

    live = counts[0]

    def split_keys(head):
        x = wide[pl.ds(head, cap, stride=2), :]
        index = lax.broadcasted_iota(jnp.int32, (cap, hd), 0)
        return jnp.where(index < live, x, x[0:1, :]).astype(jnp.bfloat16)

    def split_values(head, store):
        for c in range(cap // 128):
            x = wide[pl.ds(c * 256 + head, 128, stride=2), :]
            column = lax.broadcasted_iota(jnp.int32, (hd, 128), 1) + c * 128
            store(c, jnp.where(column < live, x.T, 0.0).astype(jnp.bfloat16))

    def live_rows():
        row = lax.broadcasted_iota(jnp.int32, (EXT, cap), 0)
        column = lax.broadcasted_iota(jnp.int32, (EXT, cap), 1)
        return jnp.where((row == 0) & (column < live), 1.0, 0.0).astype(jnp.bfloat16)

    def x_copy(n):
        src, dst = ((k_send, k_buf), (v_send, v_buf))[n]
        return pltpu.make_async_remote_copy(
            src_ref=src, dst_ref=dst.at[g], send_sem=x_send.at[n], recv_sem=x_recv.at[n],
            device_id=other, device_id_type=MESH,
        )

    load_k.wait()
    wide[0 : cap * 2, :] = raw_k[...].astype(jnp.float32)
    k_send[...] = split_keys(1 - g)
    x_copy(0).start()
    k_buf[g] = split_keys(g)

    load_v.wait()
    wide[0 : cap * 2, :] = raw_v[...].astype(jnp.float32)

    def to_send(c, x):
        v_send[0:hd, c * 128 : (c + 1) * 128] = x

    def to_own(c, x):
        v_buf[g, 0:hd, c * 128 : (c + 1) * 128] = x

    split_values(1 - g, to_send)
    v_send[hd : hd + EXT, :] = live_rows()
    x_copy(1).start()
    split_values(g, to_own)
    v_buf[g, hd : hd + EXT, :] = live_rows()

    nh = new_raw.shape[1] // tok

    def n_copy(n, dj, di):
        gg, yy = peer(dj, di)
        slot = ((ny - dj) % ny) * 2 + g
        return pltpu.make_async_remote_copy(
            src_ref=new_send.at[n], dst_ref=new_buf.at[slot],
            send_sem=n_send.at[n], recv_sem=n_recv.at[slot],
            device_id=(chip0 + gg, yy), device_id_type=MESH,
        )

    load_nk.wait()
    load_nv.wait()
    for kind in range(2):
        wide[pl.ds(kind * tok * nh, tok * nh), :] = new_raw[kind].astype(jnp.float32)
    for n, (dj, di) in enumerate(peers):
        gg, yy = peer(dj, di)
        for kind in range(2):
            new_send[n, kind] = wide[pl.ds(kind * tok * nh + 2 * yy + gg, tok, stride=nh), :].astype(jnp.bfloat16)
        n_copy(n, dj, di).start()
    for kind in range(2):
        new_buf[g, kind] = wide[pl.ds(kind * tok * nh + 2 * y + g, tok, stride=nh), :].astype(jnp.bfloat16)

    def scores(qa, t, seg, kk):
        qq = qall[qa, t * (tok // 2) : (t + 1) * (tok // 2)].reshape(half, hd)
        return dot(k_buf[seg, kk, :], qq, 1, 1)

    def fold(chunk):
        return jnp.max(chunk.reshape(KC // 8, 8, half), axis=0)

    def first(qa, seg, s_ref, m_ref):
        for t in range(2):
            cols = slice(t * half, (t + 1) * half)
            top = None
            for c in range(cap // KC):
                kk = slice(c * KC, (c + 1) * KC)
                s = scores(qa, t, seg, kk)
                s_ref[kk, cols] = s
                top = fold(s) if top is None else jnp.maximum(top, fold(s))
            m_ref[:, cols] = jnp.broadcast_to(jnp.max(top, axis=0, keepdims=True), (8, half))

    def both(qa, seg, s_new, m_new, s_old, m_old, seg_old, acc):
        for t in range(2):
            cols = slice(t * half, (t + 1) * half)
            p_ref = (p0, p1)[t]
            old = m_old[0:1, cols]
            top = None
            for c in range(cap // KC):
                kk = slice(c * KC, (c + 1) * KC)
                s = scores(qa, t, seg, kk)
                s_new[kk, cols] = s
                top = fold(s) if top is None else jnp.maximum(top, fold(s))
                p_ref[kk, :] = jnp.exp2((s_old[kk, cols] - old) * scale).astype(jnp.bfloat16)
            m_new[:, cols] = jnp.broadcast_to(jnp.max(top, axis=0, keepdims=True), (8, half))
            acc[:, cols] = dot(v_buf[seg_old], p_ref[...], 1, 0)

    def log2(x):
        return jnp.log(x) * LOG2E

    steps = len(ORDER)
    kinds = [k for k, _ in ORDER]
    sources = [j for _, j in ORDER]
    qa_of = [{"X": 2 * j, "Y": 2 * j + 1, "Z": 2 * (ny + j)}[k] for k, j in ORDER]
    qb_of = [{"X": 2 * (ny + j) + 1, "Y": 2 * j + 1, "Z": 2 * (ny + j)}[k] for k, j in ORDER]
    part_of = [{"X": 2 * j + 1, "Y": 0, "Z": 2 * j}[k] for k, j in ORDER]
    finish = [e for p in range(steps) for e in FINISH.get(p, [])]
    ends = [sum(len(FINISH.get(r, [])) for r in range(p + 1)) for p in range(steps)]
    begins = [0] + ends[:-1]
    final_slot = [2 * j + i for i, j in finish]
    final_res = [2 * ORDER.index(("X", j)) if i == 0 else 2 * ORDER.index(("Y", j)) + 1 for i, j in finish]

    def r_copy(p):
        slot = look(p, part_of)
        return pltpu.make_async_remote_copy(
            src_ref=res.at[2 * p + 1], dst_ref=part_in.at[slot],
            send_sem=r_send.at[slot], recv_sem=r_recv.at[slot],
            device_id=(next0 + g, y), device_id_type=MESH,
        )

    def r_wait(slot):
        pltpu.make_async_remote_copy(
            src_ref=part_in.at[slot], dst_ref=part_in.at[slot],
            send_sem=r_send.at[slot], recv_sem=r_recv.at[slot],
            device_id=other, device_id_type=MESH,
        ).wait_recv()

    own_heads = heads_of(g, y)
    own_block = 2 * y + g

    def o_remote(slot, tile, yy):
        return pltpu.make_async_remote_copy(
            src_ref=o_stage.at[slot], dst_ref=o_out.at[:, own_heads, :],
            send_sem=o_send.at[slot], recv_sem=o_recv.at[own_block],
            device_id=(chip0 + tile, yy), device_id_type=MESH,
        )

    def l_remote(slot, tile, yy):
        return pltpu.make_async_remote_copy(
            src_ref=lse_stage.at[slot], dst_ref=lse_out.at[own_block],
            send_sem=l_send.at[slot], recv_sem=l_recv.at[own_block],
            device_id=(chip0 + tile, yy), device_id_type=MESH,
        )

    def o_local(slot):
        return pltpu.make_async_copy(o_stage.at[slot], o_out.at[:, own_heads, :], o_send.at[slot])

    def l_local(slot):
        return pltpu.make_async_copy(lse_stage.at[slot], lse_out.at[own_block], l_send.at[slot])

    def finish_block(e, carry):
        slot = look(e, final_slot)
        src = look(e, final_res)
        tile = lax.rem(slot, 2)
        yy = lax.rem(y + lax.div(slot, 2), ny)
        r_wait(slot)
        queries = qall[slot].reshape(rows, hd)
        keys = jnp.concatenate([new_buf[2 * j + tile, 0] for j in range(ny)], axis=0)
        vals = jnp.concatenate([new_buf[2 * j + tile, 1] for j in range(ny)], axis=0)
        s = dot(keys, queries, 1, 1)
        key_row = lax.broadcasted_iota(jnp.int32, s.shape, 0)
        key_pos = lax.rem(lax.div(key_row, tok) + y, ny) * tok + lax.rem(key_row, tok)
        token = lax.div(lax.broadcasted_iota(jnp.int32, s.shape, 1), grp) + yy * tok
        s = jnp.where(key_pos <= token, s, NEG)
        top = jnp.max(s, axis=0, keepdims=True)
        p = jnp.exp2((s - top) * scale)
        total = jnp.sum(p, axis=0, keepdims=True)
        mix = dot(vals, p.astype(jnp.bfloat16), 0, 0)
        e0 = top * scale
        e1 = unpack_log(res[src, hd : hd + EXT, :])
        e2 = unpack_log(part_in[slot, hd : hd + EXT, :])
        high = jnp.maximum(e0, jnp.maximum(e1, e2))
        w0 = jnp.exp2(e0 - high)
        w1 = jnp.exp2(e1 - high)
        w2 = jnp.exp2(e2 - high)
        whole = w0 * total + w1 + w2
        inv = 1.0 / whole
        out = mix * (w0 * inv)
        out += res[src, 0:hd, :].astype(jnp.float32) * (w1 * inv)
        out += part_in[slot, 0:hd, :].astype(jnp.float32) * (w2 * inv)
        o_stage[slot] = out.T.astype(jnp.bfloat16).reshape(tok, grp, hd)
        lse_stage[slot] = jnp.broadcast_to((high + log2(whole)) * (1.0 / LOG2E), (8, rows))
        mine = slot == g

        @pl.when(mine)
        def _():
            o_local(slot).start()
            l_local(slot).start()

        @pl.when(jnp.logical_not(mine))
        def _():
            o_remote(slot, tile, yy).start()
            l_remote(slot, tile, yy).start()

        return carry

    load_q.wait()
    q_wait(1 - g)
    x_copy(0).wait_recv()
    first(qa_of[0], 0, s0, m0)
    q_wait(qb_of[0])
    for dj, di in peers:
        slot = 2 * dj + lax.rem(g + di, 2)
        pltpu.make_async_remote_copy(
            src_ref=new_buf.at[slot], dst_ref=new_buf.at[slot],
            send_sem=n_send.at[0], recv_sem=n_recv.at[slot], device_id=other, device_id_type=MESH,
        ).wait_recv()
    x_copy(1).wait_recv()

    def step(p, carry):
        later = lax.rem(p + 1, steps)
        qb = look(p, qb_of)
        qa_later = look(later, qa_of)
        kind_x = look(p, [int(k == "X") for k in kinds])
        top_a = m0[0:1, :] * scale
        both(qb, 1, s1, m1, s0, m0, 0, acc_a)
        total_a = acc_a[hd : hd + 1, :]
        ea = top_a + log2(total_a)
        res[2 * p, 0:hd, :] = (acc_a[0:hd, :] * (1.0 / total_a)).astype(jnp.bfloat16)
        res[2 * p, hd : hd + EXT, :] = pack_log(ea)

        for at, js in FORWARD.items():
            if js:

                @pl.when(p == at)
                def _(js=js):
                    for j in js:
                        for i in (1, 0):
                            q_wait(2 * j + i)
                            forward_copy(2 * j + i).start()

        for at in range(steps - 1):
            kind, j = ORDER[at + 1]
            if kind in "XZ":

                @pl.when(p == at)
                def _(slot=qb_of[at + 1]):
                    q_wait(slot)

        top_b = m1[0:1, :] * scale
        both(qa_later, 0, s0, m0, s1, m1, 1, acc_b)
        total_b = acc_b[hd : hd + 1, :]
        eb = top_b + log2(total_b)
        ea = ea + jnp.where(kind_x == 1, NEG, 0.0)
        high = jnp.maximum(ea, eb)
        wa = jnp.exp2(ea - high)
        wb = jnp.exp2(eb - high)
        whole = wa + wb
        merged = acc_a[0:hd, :] * (wa / (whole * total_a)) + acc_b[0:hd, :] * (wb / (whole * total_b))
        res[2 * p + 1, 0:hd, :] = merged.astype(jnp.bfloat16)
        res[2 * p + 1, hd : hd + EXT, :] = pack_log(high + log2(whole))

        @pl.when(look(p, [int(k != "Y") for k in kinds]) == 1)
        def _():
            r_copy(p).start()

        lax.fori_loop(look(p, begins), look(p, ends), finish_block, 0)
        return carry

    lax.fori_loop(0, steps, step, 0)

    for n, (dj, di) in enumerate(peers):
        q_copy(n, dj, di).wait_send()
        n_copy(n, dj, di).wait_send()
    for i in range(2):
        z_copy(i).wait_send()
        x_copy(i).wait_send()
    for slot in range(2, 2 * ny):
        forward_copy(slot).wait_send()
    for p, (kind, j) in enumerate(ORDER):
        if kind != "Y":
            r_copy(p).wait_send()
    for slot in range(2 * ny):
        tile, yy = slot % 2, lax.rem(y + slot // 2, ny)
        if slot < 2:

            @pl.when(g == slot)
            def _():
                o_local(slot).wait()
                l_local(slot).wait()

            @pl.when(g != slot)
            def _():
                o_remote(slot, tile, yy).wait_send()
                l_remote(slot, tile, yy).wait_send()
        else:
            o_remote(slot, tile, yy).wait_send()
            l_remote(slot, tile, yy).wait_send()
    for dj, di in peers:
        gg, yy = peer(dj, di)
        block = 2 * yy + gg
        pltpu.make_async_remote_copy(
            src_ref=o_stage.at[0], dst_ref=o_out.at[:, heads_of(gg, yy), :],
            send_sem=o_send.at[0], recv_sem=o_recv.at[block], device_id=other, device_id_type=MESH,
        ).wait_recv()
        pltpu.make_async_remote_copy(
            src_ref=lse_stage.at[0], dst_ref=lse_out.at[block],
            send_sem=l_send.at[0], recv_sem=l_recv.at[block], device_id=other, device_id_type=MESH,
        ).wait_recv()


def body(queries, cache_keys, cache_values, new_keys, new_values, counts):
    nb, ny = lax.axis_size("blk"), lax.axis_size("kv")
    tok, nq, hd = queries.shape
    cap, kvl, _ = cache_keys.shape
    nh = new_keys.shape[1]
    grp = nq // nh
    rows = tok * grp
    bf16, f32 = jnp.bfloat16, jnp.float32
    vmem, dma = pltpu.VMEM, pltpu.SemaphoreType.DMA
    any_space = pl.BlockSpec(memory_space=pl.ANY)
    steps, own = len(ORDER), 2 * ny
    attended, lse = pl.pallas_call(
        functools.partial(kernel, nb, ny),
        out_shape=(
            jax.ShapeDtypeStruct((tok, nq, hd), bf16),
            jax.ShapeDtypeStruct((own, 8, rows), f32),
        ),
        in_specs=[pl.BlockSpec(memory_space=pltpu.SMEM)] + [any_space] * 5,
        out_specs=(any_space, any_space),
        scratch_shapes=[
            vmem((cap * kvl, hd), bf16), vmem((cap * kvl, hd), bf16), vmem((cap * kvl + 16, hd), f32),
            vmem((2, cap, hd), bf16), vmem((2, hd + EXT, cap), bf16),
            vmem((cap, hd), bf16), vmem((hd + EXT, cap), bf16),
            vmem((2 * own, tok, grp, hd), bf16),
            vmem((2, tok * nh, hd), bf16), vmem((own - 1, 2, tok, hd), bf16), vmem((own, 2, tok, hd), bf16),
            vmem((cap, rows), f32), vmem((cap, rows), f32), vmem((8, rows), f32), vmem((8, rows), f32),
            vmem((cap, rows // 2), bf16), vmem((cap, rows // 2), bf16),
            vmem((hd + EXT, rows), f32), vmem((hd + EXT, rows), f32),
            vmem((2 * steps, hd + EXT, rows), bf16), vmem((own, hd + EXT, rows), bf16),
            vmem((own, tok, grp, hd), bf16), vmem((own, 8, rows), f32),
            dma((4,)), dma((own - 1,)), dma((2 * own,)), dma((2,)), dma((own,)), dma((own - 1,)), dma((own,)),
            dma((2,)), dma((2,)), dma((own,)), dma((own,)), dma((own,)), dma((own,)), dma((own,)), dma((own,)),
        ],
        compiler_params=pltpu.CompilerParams(
            collective_id=0, has_side_effects=True, vmem_limit_bytes=56 * 2**20
        ),
    )(
        counts, queries, cache_keys.reshape(cap * kvl, hd), cache_values.reshape(cap * kvl, hd),
        new_keys.reshape(tok * nh, hd), new_values.reshape(tok * nh, hd),
    )
    logsum = lse[:, 0, :].reshape(own, tok, grp).transpose(1, 0, 2).reshape(tok, nq)
    return attended, logsum


def solution(mesh):
    in_specs = (
        P(("blk", "kv"), None, None),
        P("blk", "kv", None),
        P("blk", "kv", None),
        P(("blk", "kv"), None, None),
        P(("blk", "kv"), None, None),
        P("blk"),
    )
    out_specs = (P(("blk", "kv"), None, None), P(("blk", "kv"), None))
    return jax.shard_map(body, mesh=mesh, in_specs=in_specs, out_specs=out_specs, check_vma=False)
```

```python
import functools
import math

import jax
import jax.numpy as jnp
from jax import lax
from jax.experimental import pallas as pl
from jax.experimental.pallas import tpu as pltpu
from jax.sharding import PartitionSpec as P

MESH = pl.DeviceIdType.MESH
LOG2E = math.log2(math.e)
NEG = -1e30
KC = 256
EXT = 16

ORDER = (
    ("Y", 0), ("X", 0), ("Y", 1), ("Z", 0), ("X", 1), ("Z", 1),
    ("X", 2), ("Z", 2), ("Y", 2), ("X", 3), ("Z", 3), ("Y", 3),
)
FINISH = {4: (1, 0), 6: (0, 0), 7: (1, 1), 8: (0, 1), 9: (1, 2), 10: (0, 2)}
FINISH_LAST = ((1, 3), (0, 3))
FORWARD = {0: (1, 1), 1: (1, 0), 2: (2, 1), 3: (2, 0), 5: (3, 1), 6: (3, 0)}


def look(position, values):
    result = jnp.int32(values[-1])
    for i in reversed(range(len(values) - 1)):
        result = jnp.where(position == i, jnp.int32(values[i]), result)
    return result


def dot(a, b, ca, cb):
    return lax.dot_general(a, b, (((ca,), (cb,)), ((), ())), preferred_element_type=jnp.float32)


def pack_log(value):
    hi = value.astype(jnp.bfloat16).astype(jnp.float32)
    mid = (value - hi).astype(jnp.bfloat16).astype(jnp.float32)
    low = value - hi - mid
    row = lax.broadcasted_iota(jnp.int32, (EXT, value.shape[1]), 0)
    packed = jnp.where(row == 0, hi, jnp.where(row == 1, mid, jnp.where(row == 2, low, 0.0)))
    return packed.astype(jnp.bfloat16)


def unpack_log(rows):
    wide = rows.astype(jnp.float32)
    return wide[0:1] + wide[1:2] + wide[2:3]


def kernel(
    nb, ny,
    counts, q_in, ck_in, cv_in, nk_in, nv_in,
    o_out, lse_out,
    raw_k, raw_v, wide, k_buf, v_buf, k_send, v_send, qall, new_raw, new_send, new_buf,
    s0, s1, m0, m1, p0, p1, acc_a, acc_b, res, part_in, o_stage, lse_stage,
    load_sem, q_send, q_recv, z_send, f_send, n_send, n_recv, x_send, x_recv,
    r_send, r_recv, o_send, o_recv, l_send, l_recv,
):
    cap = k_buf.shape[1]
    tok, grp, hd = qall.shape[1:]
    rows = tok * grp
    half = rows // 2
    scale = LOG2E / math.sqrt(hd)

    b = lax.axis_index("blk")
    y = lax.axis_index("kv")
    g = lax.rem(b, 2)
    chip0 = b - g
    prev0 = lax.rem(chip0 + nb - 2, nb)
    next0 = lax.rem(chip0 + 2, nb)
    other = (chip0 + 1 - g, y)

    peers = [(0, 1 - g)] + [(dj, gg) for dj in range(1, ny) for gg in range(2)]

    def row(dj):
        return lax.rem(y + dj, ny)

    def source(j):
        return lax.rem(ny + (1 - 2 * g) * j, ny)

    load_k = pltpu.make_async_copy(ck_in, raw_k, load_sem.at[0])
    load_v = pltpu.make_async_copy(cv_in, raw_v, load_sem.at[1])
    load_nk = pltpu.make_async_copy(nk_in, new_raw.at[0], load_sem.at[2])
    load_nv = pltpu.make_async_copy(nv_in, new_raw.at[1], load_sem.at[3])
    load_k.start()
    load_nk.start()
    load_nv.start()
    load_v.start()

    def heads_of(gg, yy):
        return pl.ds(pl.multiple_of((2 * yy + gg) * grp, grp), grp)

    load_q = pltpu.make_async_copy(q_in.at[:, heads_of(g, y), :], qall.at[g], q_recv.at[g])
    load_q.start()

    def q_copy(dj, gg):
        slot = ((ny - dj) % ny) * 2 + g
        return pltpu.make_async_remote_copy(
            src_ref=q_in.at[:, heads_of(gg, row(dj)), :], dst_ref=qall.at[slot],
            send_sem=q_send.at[2 * dj + gg], recv_sem=q_recv.at[slot],
            device_id=(chip0 + gg, row(dj)), device_id_type=MESH,
        )

    def z_copy(gg):
        slot = 2 * ny + g
        return pltpu.make_async_remote_copy(
            src_ref=q_in.at[:, heads_of(gg, y), :], dst_ref=qall.at[slot],
            send_sem=z_send.at[gg], recv_sem=q_recv.at[slot],
            device_id=(prev0 + gg, y), device_id_type=MESH,
        )

    def forward_copy(slot):
        return pltpu.make_async_remote_copy(
            src_ref=qall.at[slot], dst_ref=qall.at[2 * ny + slot],
            send_sem=f_send.at[slot], recv_sem=q_recv.at[2 * ny + slot],
            device_id=(prev0 + g, y), device_id_type=MESH,
        )

    def q_wait(slot):
        pltpu.make_async_remote_copy(
            src_ref=qall.at[slot], dst_ref=qall.at[slot],
            send_sem=f_send.at[0], recv_sem=q_recv.at[slot],
            device_id=other, device_id_type=MESH,
        ).wait_recv()

    barrier = pltpu.get_barrier_semaphore()
    for dj, gg in peers:
        pl.semaphore_signal(barrier, inc=1, device_id=(chip0 + gg, row(dj)), device_id_type=MESH)
    for base in (prev0, next0):
        for i in range(2):
            pl.semaphore_signal(barrier, inc=1, device_id=(base + i, y), device_id_type=MESH)

    live = counts[0]

    def x_copy(n):
        src, dst = ((k_send, k_buf), (v_send, v_buf))[n]
        return pltpu.make_async_remote_copy(
            src_ref=src, dst_ref=dst.at[g], send_sem=x_send.at[n], recv_sem=x_recv.at[n],
            device_id=other, device_id_type=MESH,
        )

    load_k.wait()
    top_rows = raw_k[0:16, :].astype(jnp.float32)
    first_keys = [jnp.where(head == 0, top_rows[0:1], top_rows[1:2]) for head in (1 - g, g)]

    def split_keys(c, carry):
        at = pl.multiple_of(c * KC, KC)
        wide[pl.ds(2 * at, 2 * KC), :] = raw_k[pl.ds(2 * at, 2 * KC), :].astype(jnp.float32)
        index = lax.broadcasted_iota(jnp.int32, (KC, hd), 0) + at
        for n, head in enumerate((1 - g, g)):
            x = wide[pl.ds(2 * at + head, KC, stride=2), :]
            x = jnp.where(index < live, x, first_keys[n]).astype(jnp.bfloat16)
            if n == 0:
                k_send[pl.ds(at, KC), :] = x
            else:
                k_buf[g, pl.ds(at, KC), :] = x
        return carry

    lax.fori_loop(0, cap // KC, split_keys, 0)
    load_v.wait()

    def split_values(c, carry):
        at = pl.multiple_of(c * KC, KC)
        wide[pl.ds(2 * at, 2 * KC), :] = raw_v[pl.ds(2 * at, 2 * KC), :].astype(jnp.float32)
        column = lax.broadcasted_iota(jnp.int32, (hd, KC), 1) + at
        mark_row = lax.broadcasted_iota(jnp.int32, (EXT, KC), 0)
        mark_column = lax.broadcasted_iota(jnp.int32, (EXT, KC), 1) + at
        marks = jnp.where((mark_row == 0) & (mark_column < live), 1.0, 0.0).astype(jnp.bfloat16)
        for n, head in enumerate((1 - g, g)):
            x = wide[pl.ds(2 * at + head, KC, stride=2), :]
            x = jnp.where(column < live, x.T, 0.0).astype(jnp.bfloat16)
            if n == 0:
                v_send[0:hd, pl.ds(at, KC)] = x
                v_send[hd : hd + EXT, pl.ds(at, KC)] = marks
            else:
                v_buf[g, 0:hd, pl.ds(at, KC)] = x
                v_buf[g, hd : hd + EXT, pl.ds(at, KC)] = marks
        return carry

    lax.fori_loop(0, cap // KC, split_values, 0)

    nh = new_raw.shape[1] // tok

    def n_copy(dj, gg):
        slot = ((ny - dj) % ny) * 2 + g
        n = 2 * dj + gg
        return pltpu.make_async_remote_copy(
            src_ref=new_send.at[n], dst_ref=new_buf.at[slot],
            send_sem=n_send.at[n], recv_sem=n_recv.at[slot],
            device_id=(chip0 + gg, row(dj)), device_id_type=MESH,
        )

    load_nk.wait()
    load_nv.wait()
    for kind in range(2):
        wide[kind * tok * nh : (kind + 1) * tok * nh, :] = new_raw[kind].astype(jnp.float32)
    for kind in range(2):
        for dj in range(ny):
            for gg in range(2):
                head = 2 * row(dj) + gg
                x = wide[pl.ds(kind * tok * nh + head, tok, stride=nh), :].astype(jnp.bfloat16)
                new_send[2 * dj + gg, kind] = x
        new_buf[g, kind] = new_send[g, kind]

    pl.semaphore_wait(barrier, len(peers) + 4)
    x_copy(0).start()
    q_copy(0, 1 - g).start()

    @pl.when(g == 1)
    def _():
        z_copy(0).start()
        z_copy(1).start()

    x_copy(1).start()
    for dj, gg in peers:
        n_copy(dj, gg).start()

    q_copy(ny - 1, 0).start()
    q_copy(1, 1).start()

    def scores(qa, t, seg, kk):
        qq = qall[qa, t * (tok // 2) : (t + 1) * (tok // 2)].reshape(half, hd)
        return dot(k_buf[seg, kk, :], qq, 1, 1)

    def fold(chunk):
        return jnp.max(chunk.reshape(KC // 8, 8, half), axis=0)

    def first(qa, seg, s_ref, m_ref):
        for t in range(2):
            cols = slice(t * half, (t + 1) * half)
            top = None
            for c in range(cap // KC):
                kk = slice(c * KC, (c + 1) * KC)
                s = scores(qa, t, seg, kk)
                s_ref[kk, cols] = s
                top = fold(s) if top is None else jnp.maximum(top, fold(s))
            m_ref[:, cols] = jnp.broadcast_to(jnp.max(top, axis=0, keepdims=True), (8, half))

    def both(qa, seg, s_new, m_new, s_old, m_old, seg_old, acc):
        for t in range(2):
            cols = slice(t * half, (t + 1) * half)
            p_ref = (p0, p1)[t]
            old = m_old[0:1, cols]
            top = None
            for c in range(cap // KC):
                kk = slice(c * KC, (c + 1) * KC)
                s = scores(qa, t, seg, kk)
                s_new[kk, cols] = s
                top = fold(s) if top is None else jnp.maximum(top, fold(s))
                p_ref[kk, :] = jnp.exp2((s_old[kk, cols] - old) * scale).astype(jnp.bfloat16)
            m_new[:, cols] = jnp.broadcast_to(jnp.max(top, axis=0, keepdims=True), (8, half))
            acc[:, cols] = dot(v_buf[seg_old], p_ref[...], 1, 0)

    def log2(x):
        return jnp.log(x) * LOG2E

    steps = len(ORDER)
    kinds = [k for k, _ in ORDER]
    sources = [j for _, j in ORDER]
    own = 2 * ny
    base_a = [{"X": 0, "Y": 1, "Z": own}[k] for k in kinds]
    base_b = [{"X": own + 1, "Y": 1, "Z": own}[k] for k in kinds]
    part_tile = [int(k == "X") for k in kinds]

    def qa_at(p):
        return look(p, base_a) + 2 * source(look(p, sources))

    def qb_at(p):
        return look(p, base_b) + 2 * source(look(p, sources))

    at_steps = [FINISH.get(p, (0, 0)) for p in range(steps)]

    def r_copy(p):
        slot = look(p, part_tile) + 2 * source(look(p, sources))
        return pltpu.make_async_remote_copy(
            src_ref=res.at[2 * p + 1], dst_ref=part_in.at[slot],
            send_sem=r_send.at[slot], recv_sem=r_recv.at[slot],
            device_id=(next0 + g, y), device_id_type=MESH,
        )

    def r_wait(slot):
        pltpu.make_async_remote_copy(
            src_ref=part_in.at[slot], dst_ref=part_in.at[slot],
            send_sem=r_send.at[slot], recv_sem=r_recv.at[slot],
            device_id=other, device_id_type=MESH,
        ).wait_recv()

    own_heads = heads_of(g, y)
    own_block = 2 * y + g

    def o_remote(slot, tile, yy):
        return pltpu.make_async_remote_copy(
            src_ref=o_stage.at[slot], dst_ref=o_out.at[:, own_heads, :],
            send_sem=o_send.at[slot], recv_sem=o_recv.at[own_block],
            device_id=(chip0 + tile, yy), device_id_type=MESH,
        )

    def l_remote(slot, tile, yy):
        return pltpu.make_async_remote_copy(
            src_ref=lse_stage.at[slot], dst_ref=lse_out.at[own_block],
            send_sem=l_send.at[slot], recv_sem=l_recv.at[own_block],
            device_id=(chip0 + tile, yy), device_id_type=MESH,
        )

    def o_local(slot):
        return pltpu.make_async_copy(o_stage.at[slot], o_out.at[:, own_heads, :], o_send.at[slot])

    def l_local(slot):
        return pltpu.make_async_copy(lse_stage.at[slot], lse_out.at[own_block], l_send.at[slot])

    def slot_of(tile, j):
        return 2 * source(j) + tile

    def finish_math(slot, src, part, stage):
        tile = lax.rem(slot, 2)
        yy = lax.rem(y + lax.div(slot, 2), ny)
        queries = qall[slot].reshape(rows, hd)
        keys = jnp.concatenate([new_buf[2 * j + tile, 0] for j in range(ny)], axis=0)
        vals = jnp.concatenate([new_buf[2 * j + tile, 1] for j in range(ny)], axis=0)
        s = dot(keys, queries, 1, 1)
        key_row = lax.broadcasted_iota(jnp.int32, s.shape, 0)
        key_pos = lax.rem(lax.div(key_row, tok) + y, ny) * tok + lax.rem(key_row, tok)
        token = lax.div(lax.broadcasted_iota(jnp.int32, s.shape, 1), grp) + yy * tok
        s = jnp.where(key_pos <= token, s, NEG)
        top = jnp.max(s, axis=0, keepdims=True)
        p = jnp.exp2((s - top) * scale)
        total = jnp.sum(p, axis=0, keepdims=True)
        mix = dot(vals, p.astype(jnp.bfloat16), 0, 0)
        e0 = top * scale
        e1 = unpack_log(res[src, hd : hd + EXT, :])
        e2 = unpack_log(part_in[part, hd : hd + EXT, :])
        high = jnp.maximum(e0, jnp.maximum(e1, e2))
        w0 = jnp.exp2(e0 - high)
        w1 = jnp.exp2(e1 - high)
        w2 = jnp.exp2(e2 - high)
        whole = w0 * total + w1 + w2
        inv = 1.0 / whole
        out = mix * (w0 * inv)
        out += res[src, 0:hd, :].astype(jnp.float32) * (w1 * inv)
        out += part_in[part, 0:hd, :].astype(jnp.float32) * (w2 * inv)
        o_stage[stage] = out.T.astype(jnp.bfloat16).reshape(tok, grp, hd)
        lse_stage[stage] = jnp.broadcast_to((high + log2(whole)) * (1.0 / LOG2E), (8, rows))

    def finish_send(slot):
        tile = lax.rem(slot, 2)
        yy = lax.rem(y + lax.div(slot, 2), ny)
        mine = slot == g

        @pl.when(mine)
        def _():
            o_local(slot).start()
            l_local(slot).start()

        @pl.when(jnp.logical_not(mine))
        def _():
            o_remote(slot, tile, yy).start()
            l_remote(slot, tile, yy).start()

    def state_of(tile, j):
        return 2 * ORDER.index(("X", j)) if tile == 0 else 2 * ORDER.index(("Y", j)) + 1

    load_q.wait()
    q_wait(1 - g)
    x_copy(0).wait_recv()
    first(qa_at(0), 0, s0, m0)

    @pl.when(g == 0)
    def _():
        z_copy(0).start()
        z_copy(1).start()

    for dj in range(2, ny - 1):
        for gg in range(2):
            q_copy(dj, gg).start()
    for dj, gg in peers:
        slot = 2 * dj + gg
        pltpu.make_async_remote_copy(
            src_ref=new_buf.at[slot], dst_ref=new_buf.at[slot],
            send_sem=n_send.at[0], recv_sem=n_recv.at[slot], device_id=other, device_id_type=MESH,
        ).wait_recv()
    x_copy(1).wait_recv()

    def block_at(p):
        return look(p, [i for i, _ in at_steps]) + 2 * source(look(p, [j for _, j in at_steps]))

    def step(p, carry):
        later = lax.rem(p + 1, steps)
        kind_x = look(p, [int(k == "X") for k in kinds])
        ends_block = look(p, [int(q in FINISH) for q in range(steps)]) == 1
        done = block_at(p)
        done_state = look(p, [state_of(i, j) for i, j in at_steps])

        spare = jnp.where(ends_block, done, own)
        finish_math(done, done_state, spare, spare)
        top_a = m0[0:1, :] * scale
        both(qb_at(p), 1, s1, m1, s0, m0, 0, acc_a)
        total_a = acc_a[hd : hd + 1, :]
        ea = top_a + log2(total_a)
        res[2 * p, 0:hd, :] = (acc_a[0:hd, :] * (1.0 / total_a)).astype(jnp.bfloat16)
        res[2 * p, hd : hd + EXT, :] = pack_log(ea)
        top_b = m1[0:1, :] * scale
        both(qa_at(later), 0, s0, m0, s1, m1, 1, acc_b)
        total_b = acc_b[hd : hd + 1, :]
        eb = top_b + log2(total_b)
        ea = ea + jnp.where(kind_x == 1, NEG, 0.0)
        high = jnp.maximum(ea, eb)
        wa = jnp.exp2(ea - high)
        wb = jnp.exp2(eb - high)
        whole = wa + wb
        merged = acc_a[0:hd, :] * (wa / (whole * total_a)) + acc_b[0:hd, :] * (wb / (whole * total_b))
        res[2 * p + 1, 0:hd, :] = merged.astype(jnp.bfloat16)
        res[2 * p + 1, hd : hd + EXT, :] = pack_log(high + log2(whole))

        @pl.when(look(p, [int(k != "Y") for k in kinds]) == 1)
        def _():
            r_copy(p).start()

        @pl.when(ends_block)
        def _():
            finish_send(done)

        @pl.when(look(p, [int(at in FORWARD) for at in range(steps)]) == 1)
        def _():
            entries = [FORWARD.get(at, (0, 0)) for at in range(steps)]
            slot = 2 * source(look(p, [j for j, _ in entries])) + look(p, [i for _, i in entries])
            q_wait(slot)
            forward_copy(slot).start()

        @pl.when(p == 1)
        def _():
            q_copy(ny - 1, 1).start()
            q_copy(1, 0).start()

        @pl.when(look(p, [int(k == "X") for k in kinds[1:]] + [0]) == 1)
        def _():
            q_wait(qb_at(p + 1))

        @pl.when(look(p, [int(k == "Z") for k in kinds[2:]] + [0, 0]) == 1)
        def _():
            q_wait(qa_at(p + 2))

        @pl.when(look(p, [int(q + 1 in FINISH) for q in range(steps)]) == 1)
        def _():
            r_wait(block_at(p + 1))

        return carry

    lax.fori_loop(0, steps, step, 0)

    def last(n, carry):
        slot = look(n, [i for i, _ in FINISH_LAST]) + 2 * source(look(n, [j for _, j in FINISH_LAST]))
        r_wait(slot)
        finish_math(slot, look(n, [state_of(i, j) for i, j in FINISH_LAST]), slot, slot)
        finish_send(slot)
        return carry

    lax.fori_loop(0, len(FINISH_LAST), last, 0)

    for dj, gg in peers:
        q_copy(dj, gg).wait_send()
        n_copy(dj, gg).wait_send()
    for i in range(2):
        z_copy(i).wait_send()
        x_copy(i).wait_send()
    for slot in range(2, 2 * ny):
        forward_copy(slot).wait_send()
    for p, (kind, j) in enumerate(ORDER):
        if kind != "Y":
            r_copy(p).wait_send()
    for slot in range(2 * ny):
        tile, yy = slot % 2, lax.rem(y + slot // 2, ny)
        if slot < 2:

            @pl.when(g == slot)
            def _():
                o_local(slot).wait()
                l_local(slot).wait()

            @pl.when(g != slot)
            def _():
                o_remote(slot, tile, yy).wait_send()
                l_remote(slot, tile, yy).wait_send()
        else:
            o_remote(slot, tile, yy).wait_send()
            l_remote(slot, tile, yy).wait_send()
    for dj, gg in peers:
        yy = row(dj)
        block = 2 * yy + gg
        pltpu.make_async_remote_copy(
            src_ref=o_stage.at[0], dst_ref=o_out.at[:, heads_of(gg, yy), :],
            send_sem=o_send.at[0], recv_sem=o_recv.at[block], device_id=other, device_id_type=MESH,
        ).wait_recv()
        pltpu.make_async_remote_copy(
            src_ref=lse_stage.at[0], dst_ref=lse_out.at[block],
            send_sem=l_send.at[0], recv_sem=l_recv.at[block], device_id=other, device_id_type=MESH,
        ).wait_recv()


def last_kernel(tok, grp, o_in, lse_in, o_out, lse_out, sem):
    copy = pltpu.make_async_copy(o_in, o_out, sem)
    copy.start()
    blocks, _, rows = lse_in.shape
    token = lax.broadcasted_iota(jnp.int32, (tok, rows), 0)
    owner = lax.div(lax.broadcasted_iota(jnp.int32, (tok, rows), 1), grp)
    head = lax.rem(lax.broadcasted_iota(jnp.int32, (rows, blocks * grp), 0), grp)
    column = lax.broadcasted_iota(jnp.int32, (rows, blocks * grp), 1)
    out = None
    for block in range(blocks):
        spread = jnp.where(token == owner, lse_in[block, 0:1, :], 0.0)
        place = (column == head + block * grp).astype(jnp.bfloat16)
        hi = spread.astype(jnp.bfloat16)
        rest = spread - hi.astype(jnp.float32)
        mid = rest.astype(jnp.bfloat16)
        low = (rest - mid.astype(jnp.float32)).astype(jnp.bfloat16)
        part = dot(hi, place, 1, 0) + (dot(mid, place, 1, 0) + dot(low, place, 1, 0))
        out = part if out is None else out + part
    lse_out[...] = out
    copy.wait()


def body(queries, cache_keys, cache_values, new_keys, new_values, counts):
    nb, ny = lax.axis_size("blk"), lax.axis_size("kv")
    tok, nq, hd = queries.shape
    cap, kvl, _ = cache_keys.shape
    nh = new_keys.shape[1]
    grp = nq // nh
    rows = tok * grp
    bf16, f32 = jnp.bfloat16, jnp.float32
    vmem, dma = pltpu.VMEM, pltpu.SemaphoreType.DMA
    any_space = pl.BlockSpec(memory_space=pl.ANY)
    steps, own = len(ORDER), 2 * ny
    attended, lse = pl.pallas_call(
        functools.partial(kernel, nb, ny),
        out_shape=(
            jax.ShapeDtypeStruct((tok, nq, hd), bf16),
            jax.ShapeDtypeStruct((own, 8, rows), f32),
        ),
        in_specs=[pl.BlockSpec(memory_space=pltpu.SMEM)] + [any_space] * 5,
        out_specs=(any_space, any_space),
        scratch_shapes=[
            vmem((cap * kvl, hd), bf16), vmem((cap * kvl, hd), bf16), vmem((cap * kvl + 16, hd), f32),
            vmem((2, cap, hd), bf16), vmem((2, hd + EXT, cap), bf16),
            vmem((cap, hd), bf16), vmem((hd + EXT, cap), bf16),
            vmem((2 * own, tok, grp, hd), bf16),
            vmem((2, tok * nh, hd), bf16), vmem((own, 2, tok, hd), bf16), vmem((own, 2, tok, hd), bf16),
            vmem((cap, rows), f32), vmem((cap, rows), f32), vmem((8, rows), f32), vmem((8, rows), f32),
            vmem((cap, rows // 2), bf16), vmem((cap, rows // 2), bf16),
            vmem((hd + EXT, rows), f32), vmem((hd + EXT, rows), f32),
            vmem((2 * steps, hd + EXT, rows), bf16), vmem((own + 1, hd + EXT, rows), bf16),
            vmem((own + 1, tok, grp, hd), bf16), vmem((own + 1, 8, rows), f32),
            dma((4,)), dma((own,)), dma((2 * own,)), dma((2,)), dma((own,)), dma((own,)), dma((own,)),
            dma((2,)), dma((2,)), dma((own,)), dma((own,)), dma((own,)), dma((own,)), dma((own,)), dma((own,)),
        ],
        compiler_params=pltpu.CompilerParams(
            collective_id=0, has_side_effects=True, vmem_limit_bytes=56 * 2**20
        ),
    )(
        counts, queries, cache_keys.reshape(cap * kvl, hd), cache_values.reshape(cap * kvl, hd),
        new_keys.reshape(tok * nh, hd), new_values.reshape(tok * nh, hd),
    )
    return pl.pallas_call(
        functools.partial(last_kernel, tok, grp),
        out_shape=(jax.ShapeDtypeStruct((tok, nq, hd), bf16), jax.ShapeDtypeStruct((tok, nq), f32)),
        in_specs=[pl.BlockSpec(memory_space=vmem)] * 2,
        out_specs=(any_space, pl.BlockSpec(memory_space=vmem)),
        scratch_shapes=[dma],
    )(attended, lse)


def solution(mesh):
    in_specs = (
        P(("blk", "kv"), None, None),
        P("blk", "kv", None),
        P("blk", "kv", None),
        P(("blk", "kv"), None, None),
        P(("blk", "kv"), None, None),
        P("blk"),
    )
    out_specs = (P(("blk", "kv"), None, None), P(("blk", "kv"), None))
    return jax.shard_map(body, mesh=mesh, in_specs=in_specs, out_specs=out_specs, check_vma=False)
```

```python
import functools
import math

import jax
import jax.numpy as jnp
from jax import lax
from jax.experimental import pallas as pl
from jax.experimental.pallas import tpu as pltpu
from jax.sharding import PartitionSpec as P

MESH = pl.DeviceIdType.MESH
LOG2E = math.log2(math.e)
NEG = -1e30
KC = 256
BETWEEN = 4
EXT = 16

ORDER = (
    ("Y", 0), ("X", 0), ("Y", 1), ("Z", 0), ("X", 1), ("Z", 1),
    ("X", 2), ("Z", 2), ("Y", 2), ("X", 3), ("Z", 3), ("Y", 3),
)
FINISH = {4: (1, 0), 6: (0, 0), 7: (1, 1), 8: (0, 1), 9: (1, 2), 10: (0, 2)}
FINISH_LAST = ((1, 3), (0, 3))
FORWARD = {0: (1, 1), 1: (1, 0), 2: (2, 1), 3: (2, 0), 5: (3, 1), 6: (3, 0)}


def look(position, values):
    result = jnp.int32(values[-1])
    for i in reversed(range(len(values) - 1)):
        result = jnp.where(position == i, jnp.int32(values[i]), result)
    return result


def dot(a, b, ca, cb):
    return lax.dot_general(a, b, (((ca,), (cb,)), ((), ())), preferred_element_type=jnp.float32)


def pack_log(value):
    hi = value.astype(jnp.bfloat16).astype(jnp.float32)
    mid = (value - hi).astype(jnp.bfloat16).astype(jnp.float32)
    low = value - hi - mid
    row = lax.broadcasted_iota(jnp.int32, (EXT, value.shape[1]), 0)
    packed = jnp.where(row == 0, hi, jnp.where(row == 1, mid, jnp.where(row == 2, low, 0.0)))
    return packed.astype(jnp.bfloat16)


def unpack_log(rows):
    wide = rows.astype(jnp.float32)
    return wide[0:1] + wide[1:2] + wide[2:3]


def kernel(
    nb, ny,
    counts, q_in, ck_in, cv_in, nk_in, nv_in,
    o_out, lse_out,
    raw_k, raw_v, wide, k_buf, v_buf, k_send, v_send, qall, new_raw, new_send, new_buf,
    s0, s1, m0, m1, p0, p1, acc_a, acc_b, dead, res, part_in, o_stage, lse_stage,
    load_sem, q_send, q_recv, z_send, f_send, n_send, n_recv, x_send, x_recv,
    r_send, r_recv, o_send, o_recv, l_send, l_recv,
):
    cap = k_buf.shape[1]
    tok, grp, hd = qall.shape[1:]
    rows = tok * grp
    half = rows // 2
    scale = LOG2E / math.sqrt(hd)

    b = lax.axis_index("blk")
    y = lax.axis_index("kv")
    g = lax.rem(b, 2)
    chip0 = b - g
    prev0 = lax.rem(chip0 + nb - 2, nb)
    next0 = lax.rem(chip0 + 2, nb)
    other = (chip0 + 1 - g, y)

    peers = [(0, 1 - g)] + [(dj, gg) for dj in range(1, ny) for gg in range(2)]

    def row(dj):
        return lax.rem(y + dj, ny)

    def source(j):
        return lax.rem(ny + (1 - 2 * g) * j, ny)

    load_k = pltpu.make_async_copy(ck_in, raw_k, load_sem.at[0])
    load_v = pltpu.make_async_copy(cv_in, raw_v, load_sem.at[1])
    load_nk = pltpu.make_async_copy(nk_in, new_raw.at[0], load_sem.at[2])
    load_nv = pltpu.make_async_copy(nv_in, new_raw.at[1], load_sem.at[3])
    load_k.start()
    load_nk.start()
    load_nv.start()
    load_v.start()

    def heads_of(gg, yy):
        return pl.ds(pl.multiple_of((2 * yy + gg) * grp, grp), grp)

    load_q = pltpu.make_async_copy(q_in.at[:, heads_of(g, y), :], qall.at[g], q_recv.at[g])
    load_q.start()

    def q_copy(dj, gg):
        slot = ((ny - dj) % ny) * 2 + g
        return pltpu.make_async_remote_copy(
            src_ref=q_in.at[:, heads_of(gg, row(dj)), :], dst_ref=qall.at[slot],
            send_sem=q_send.at[2 * dj + gg], recv_sem=q_recv.at[slot],
            device_id=(chip0 + gg, row(dj)), device_id_type=MESH,
        )

    def z_copy(gg):
        slot = 2 * ny + g
        return pltpu.make_async_remote_copy(
            src_ref=q_in.at[:, heads_of(gg, y), :], dst_ref=qall.at[slot],
            send_sem=z_send.at[gg], recv_sem=q_recv.at[slot],
            device_id=(prev0 + gg, y), device_id_type=MESH,
        )

    def forward_copy(slot):
        return pltpu.make_async_remote_copy(
            src_ref=qall.at[slot], dst_ref=qall.at[2 * ny + slot],
            send_sem=f_send.at[slot], recv_sem=q_recv.at[2 * ny + slot],
            device_id=(prev0 + g, y), device_id_type=MESH,
        )

    def q_wait(slot):
        pltpu.make_async_remote_copy(
            src_ref=qall.at[slot], dst_ref=qall.at[slot],
            send_sem=f_send.at[0], recv_sem=q_recv.at[slot],
            device_id=other, device_id_type=MESH,
        ).wait_recv()

    barrier = pltpu.get_barrier_semaphore()
    for dj, gg in peers:
        pl.semaphore_signal(barrier, inc=1, device_id=(chip0 + gg, row(dj)), device_id_type=MESH)
    for base in (prev0, next0):
        for i in range(2):
            pl.semaphore_signal(barrier, inc=1, device_id=(base + i, y), device_id_type=MESH)

    nh = new_raw.shape[1] // tok

    def n_copy(dj, gg):
        slot = ((ny - dj) % ny) * 2 + g
        n = 2 * dj + gg
        return pltpu.make_async_remote_copy(
            src_ref=new_send.at[n], dst_ref=new_buf.at[slot],
            send_sem=n_send.at[n], recv_sem=n_recv.at[slot],
            device_id=(chip0 + gg, row(dj)), device_id_type=MESH,
        )

    load_nk.wait()
    load_nv.wait()
    for kind in range(2):
        wide[kind * tok * nh : (kind + 1) * tok * nh, :] = new_raw[kind].astype(jnp.float32)
    for kind in range(2):
        for dj in range(ny):
            for gg in range(2):
                head = 2 * row(dj) + gg
                x = wide[pl.ds(kind * tok * nh + head, tok, stride=nh), :].astype(jnp.bfloat16)
                new_send[2 * dj + gg, kind] = x
        new_buf[g, kind] = new_send[g, kind]

    live = counts[0]

    def x_copy(n):
        src, dst = ((k_send, k_buf), (v_send, v_buf))[n]
        return pltpu.make_async_remote_copy(
            src_ref=src, dst_ref=dst.at[g], send_sem=x_send.at[n], recv_sem=x_recv.at[n],
            device_id=other, device_id_type=MESH,
        )

    load_k.wait()
    top_rows = raw_k[0:16, :].astype(jnp.float32)
    first_keys = [jnp.where(head == 0, top_rows[0:1], top_rows[1:2]) for head in (1 - g, g)]

    def split_keys(c, carry):
        at = pl.multiple_of(c * KC, KC)
        wide[pl.ds(2 * at, 2 * KC), :] = raw_k[pl.ds(2 * at, 2 * KC), :].astype(jnp.float32)
        index = lax.broadcasted_iota(jnp.int32, (KC, hd), 0) + at
        for n, head in enumerate((1 - g, g)):
            x = wide[pl.ds(2 * at + head, KC, stride=2), :]
            x = jnp.where(index < live, x, first_keys[n]).astype(jnp.bfloat16)
            if n == 0:
                k_send[pl.ds(at, KC), :] = x
            else:
                k_buf[g, pl.ds(at, KC), :] = x
        return carry

    lax.fori_loop(0, cap // KC, split_keys, 0)
    pl.semaphore_wait(barrier, len(peers) + 4)
    x_copy(0).start()
    q_copy(0, 1 - g).start()

    @pl.when(g == 1)
    def _():
        z_copy(0).start()
        z_copy(1).start()

    for dj, gg in peers:
        n_copy(dj, gg).start()

    q_copy(ny - 1, 0).start()
    q_copy(1, 1).start()

    load_v.wait()

    def split_values(c, carry):
        at = pl.multiple_of(c * KC, KC)
        wide[pl.ds(2 * at, 2 * KC), :] = raw_v[pl.ds(2 * at, 2 * KC), :].astype(jnp.float32)
        column = lax.broadcasted_iota(jnp.int32, (hd, KC), 1) + at
        mark_row = lax.broadcasted_iota(jnp.int32, (EXT, KC), 0)
        mark_column = lax.broadcasted_iota(jnp.int32, (EXT, KC), 1) + at
        marks = jnp.where((mark_row == 0) & (mark_column < live), 1.0, 0.0).astype(jnp.bfloat16)
        for n, head in enumerate((1 - g, g)):
            x = wide[pl.ds(2 * at + head, KC, stride=2), :]
            x = jnp.where(column < live, x.T, 0.0).astype(jnp.bfloat16)
            if n == 0:
                v_send[0:hd, pl.ds(at, KC)] = x
                v_send[hd : hd + EXT, pl.ds(at, KC)] = marks
            else:
                v_buf[g, 0:hd, pl.ds(at, KC)] = x
                v_buf[g, hd : hd + EXT, pl.ds(at, KC)] = marks
        return carry

    lax.fori_loop(0, cap // KC, split_values, 0)

    x_copy(1).start()

    def scores(qa, t, seg, kk):
        qq = qall[qa, t * (tok // 2) : (t + 1) * (tok // 2)].reshape(half, hd)
        return dot(k_buf[seg, kk, :], qq, 1, 1)

    def fold(chunk):
        return jnp.max(chunk.reshape(KC // 8, 8, half), axis=0)

    def first(qa, seg, s_ref, m_ref):
        for t in range(2):
            cols = slice(t * half, (t + 1) * half)
            top = None
            for c in range(cap // KC):
                kk = slice(c * KC, (c + 1) * KC)
                s = scores(qa, t, seg, kk)
                s_ref[kk, cols] = s
                top = fold(s) if top is None else jnp.maximum(top, fold(s))
            m_ref[:, cols] = jnp.broadcast_to(jnp.max(top, axis=0, keepdims=True), (8, half))

    def tile(t, qa, seg, s_new, m_new, s_old, m_old, seg_old, between):
        cols = slice(t * half, (t + 1) * half)
        p_ref = (p0, p1)[t]
        old = m_old[0:1, cols] * scale
        top = total = None
        for c in range(cap // KC):
            if c == BETWEEN:
                between()
            kk = slice(c * KC, (c + 1) * KC)
            s = scores(qa, t, seg, kk)
            s_new[kk, cols] = s
            top = fold(s) if top is None else jnp.maximum(top, fold(s))
            p = jnp.exp2(s_old[kk, cols] * scale - old)
            p_ref[kk, :] = p.astype(jnp.bfloat16)
            if c == 0:
                weight_0 = p[0:1, :]
            part = jnp.sum(p.reshape(KC // 8, 8, half), axis=0) - dead[seg_old, c] * weight_0
            total = part if total is None else total + part
        m_new[:, cols] = jnp.broadcast_to(jnp.max(top, axis=0, keepdims=True), (8, half))
        return jnp.sum(total, axis=0, keepdims=True)

    def mix_half(t, seg, acc):
        acc[:, t * half : (t + 1) * half] = dot(v_buf[seg, 0:hd], (p0, p1)[t][...], 1, 0)

    def log2(x):
        return jnp.log(x) * LOG2E

    steps = len(ORDER)
    kinds = [k for k, _ in ORDER]
    sources = [j for _, j in ORDER]
    own = 2 * ny
    base_a = [{"X": 0, "Y": 1, "Z": own}[k] for k in kinds]
    base_b = [{"X": own + 1, "Y": 1, "Z": own}[k] for k in kinds]
    part_tile = [int(k == "X") for k in kinds]

    def qa_at(p):
        return look(p, base_a) + 2 * source(look(p, sources))

    def qb_at(p):
        return look(p, base_b) + 2 * source(look(p, sources))

    def seg_at(p):
        return g * look(p, [int(k != "X") for k in kinds])

    at_steps = [FINISH.get(p, (0, 0)) for p in range(steps)]

    def r_copy(p):
        slot = look(p, part_tile) + 2 * source(look(p, sources))
        return pltpu.make_async_remote_copy(
            src_ref=res.at[2 * p + 1], dst_ref=part_in.at[slot],
            send_sem=r_send.at[slot], recv_sem=r_recv.at[slot],
            device_id=(next0 + g, y), device_id_type=MESH,
        )

    def r_wait(slot):
        pltpu.make_async_remote_copy(
            src_ref=part_in.at[slot], dst_ref=part_in.at[slot],
            send_sem=r_send.at[slot], recv_sem=r_recv.at[slot],
            device_id=other, device_id_type=MESH,
        ).wait_recv()

    own_heads = heads_of(g, y)
    own_block = 2 * y + g

    def o_remote(slot, tile, yy):
        return pltpu.make_async_remote_copy(
            src_ref=o_stage.at[slot], dst_ref=o_out.at[:, own_heads, :],
            send_sem=o_send.at[slot], recv_sem=o_recv.at[own_block],
            device_id=(chip0 + tile, yy), device_id_type=MESH,
        )

    def l_remote(slot, tile, yy):
        return pltpu.make_async_remote_copy(
            src_ref=lse_stage.at[slot], dst_ref=lse_out.at[own_block],
            send_sem=l_send.at[slot], recv_sem=l_recv.at[own_block],
            device_id=(chip0 + tile, yy), device_id_type=MESH,
        )

    def o_local(slot):
        return pltpu.make_async_copy(o_stage.at[slot], o_out.at[:, own_heads, :], o_send.at[slot])

    def l_local(slot):
        return pltpu.make_async_copy(lse_stage.at[slot], lse_out.at[own_block], l_send.at[slot])

    def slot_of(tile, j):
        return 2 * source(j) + tile

    def finish_math(slot, src, part, stage):
        tile = lax.rem(slot, 2)
        yy = lax.rem(y + lax.div(slot, 2), ny)
        queries = qall[slot].reshape(rows, hd)
        keys = jnp.concatenate([new_buf[2 * j + tile, 0] for j in range(ny)], axis=0)
        vals = jnp.concatenate([new_buf[2 * j + tile, 1] for j in range(ny)], axis=0)
        s = dot(keys, queries, 1, 1)
        key_row = lax.broadcasted_iota(jnp.int32, s.shape, 0)
        key_pos = lax.rem(lax.div(key_row, tok) + y, ny) * tok + lax.rem(key_row, tok)
        token = lax.div(lax.broadcasted_iota(jnp.int32, s.shape, 1), grp) + yy * tok
        s = jnp.where(key_pos <= token, s, NEG)
        top = jnp.max(s, axis=0, keepdims=True)
        p = jnp.exp2((s - top) * scale)
        total = jnp.sum(p, axis=0, keepdims=True)
        mix = dot(vals, p.astype(jnp.bfloat16), 0, 0)
        e0 = top * scale
        e1 = unpack_log(res[src, hd : hd + EXT, :])
        e2 = unpack_log(part_in[part, hd : hd + EXT, :])
        high = jnp.maximum(e0, jnp.maximum(e1, e2))
        w0 = jnp.exp2(e0 - high)
        w1 = jnp.exp2(e1 - high)
        w2 = jnp.exp2(e2 - high)
        whole = w0 * total + w1 + w2
        inv = 1.0 / whole
        out = mix * (w0 * inv)
        out += res[src, 0:hd, :].astype(jnp.float32) * (w1 * inv)
        out += part_in[part, 0:hd, :].astype(jnp.float32) * (w2 * inv)
        o_stage[stage] = out.T.astype(jnp.bfloat16).reshape(tok, grp, hd)
        lse_stage[stage] = jnp.broadcast_to((high + log2(whole)) * (1.0 / LOG2E), (8, rows))

    def finish_send(slot):
        tile = lax.rem(slot, 2)
        yy = lax.rem(y + lax.div(slot, 2), ny)
        mine = slot == g

        @pl.when(mine)
        def _():
            o_local(slot).start()
            l_local(slot).start()

        @pl.when(jnp.logical_not(mine))
        def _():
            o_remote(slot, tile, yy).start()
            l_remote(slot, tile, yy).start()

    def state_of(tile, j):
        return 2 * ORDER.index(("X", j)) if tile == 0 else 2 * ORDER.index(("Y", j)) + 1

    load_q.wait()
    q_wait(1 - g)
    first(qa_at(0), seg_at(0), s0, m0)

    @pl.when(g == 0)
    def _():
        z_copy(0).start()
        z_copy(1).start()

    for dj in range(2, ny - 1):
        for gg in range(2):
            q_copy(dj, gg).start()
    for dj, gg in peers:
        slot = 2 * dj + gg
        pltpu.make_async_remote_copy(
            src_ref=new_buf.at[slot], dst_ref=new_buf.at[slot],
            send_sem=n_send.at[0], recv_sem=n_recv.at[slot], device_id=other, device_id_type=MESH,
        ).wait_recv()
    x_copy(0).wait_recv()
    x_copy(1).wait_recv()
    for seg in range(2):
        for c in range(cap // KC):
            marks = v_buf[seg, hd : hd + EXT, c * KC : (c + 1) * KC].astype(jnp.float32)
            rows_live = jnp.sum(jnp.sum(marks, axis=0, keepdims=True), axis=1, keepdims=True)
            dead[seg, c] = jnp.broadcast_to((KC - rows_live) * 0.125, (8, half))

    def block_at(p):
        return look(p, [i for i, _ in at_steps]) + 2 * source(look(p, [j for _, j in at_steps]))

    def step(p, carry):
        later = lax.rem(p + 1, steps)
        kind_x = look(p, [int(k == "X") for k in kinds])
        ends_block = look(p, [int(q in FINISH) for q in range(steps)]) == 1
        done = block_at(p)
        done_state = look(p, [state_of(i, j) for i, j in at_steps])

        spare = jnp.where(ends_block, done, own)
        top_a = m0[0:1, :] * scale
        qb, qa = qb_at(p), qa_at(later)
        seg_a, seg_later = seg_at(p), seg_at(later)
        seg_b = 1 - seg_a
        a0 = tile(0, qb, seg_b, s1, m1, s0, m0, seg_a, lambda: finish_math(done, done_state, spare, spare))
        a1 = tile(1, qb, seg_b, s1, m1, s0, m0, seg_a, lambda: mix_half(0, seg_a, acc_a))
        top_b = m1[0:1, :] * scale
        b0 = tile(0, qa, seg_later, s0, m0, s1, m1, seg_b, lambda: mix_half(1, seg_a, acc_a))
        b1 = tile(1, qa, seg_later, s0, m0, s1, m1, seg_b, lambda: mix_half(0, seg_b, acc_b))
        mix_half(1, seg_b, acc_b)
        total_a = jnp.concatenate([a0, a1], axis=1)
        ea = top_a + log2(total_a)
        res[2 * p, 0:hd, :] = (acc_a[...] * (1.0 / total_a)).astype(jnp.bfloat16)
        res[2 * p, hd : hd + EXT, :] = pack_log(ea)
        total_b = jnp.concatenate([b0, b1], axis=1)
        eb = top_b + log2(total_b)
        ea = ea + jnp.where(kind_x == 1, NEG, 0.0)
        high = jnp.maximum(ea, eb)
        wa = jnp.exp2(ea - high)
        wb = jnp.exp2(eb - high)
        whole = wa + wb
        merged = acc_a[...] * (wa / (whole * total_a)) + acc_b[...] * (wb / (whole * total_b))
        res[2 * p + 1, 0:hd, :] = merged.astype(jnp.bfloat16)
        res[2 * p + 1, hd : hd + EXT, :] = pack_log(high + log2(whole))

        @pl.when(look(p, [int(k != "Y") for k in kinds]) == 1)
        def _():
            r_copy(p).start()

        @pl.when(ends_block)
        def _():
            finish_send(done)

        @pl.when(look(p, [int(at in FORWARD) for at in range(steps)]) == 1)
        def _():
            entries = [FORWARD.get(at, (0, 0)) for at in range(steps)]
            slot = 2 * source(look(p, [j for j, _ in entries])) + look(p, [i for _, i in entries])
            q_wait(slot)
            forward_copy(slot).start()

        @pl.when(p == 1)
        def _():
            q_copy(ny - 1, 1).start()
            q_copy(1, 0).start()

        @pl.when(look(p, [int(k == "X") for k in kinds[1:]] + [0]) == 1)
        def _():
            q_wait(qb_at(p + 1))

        @pl.when(look(p, [int(k == "Z") for k in kinds[2:]] + [0, 0]) == 1)
        def _():
            q_wait(qa_at(p + 2))

        @pl.when(look(p, [int(q + 1 in FINISH) for q in range(steps)]) == 1)
        def _():
            r_wait(block_at(p + 1))

        return carry

    lax.fori_loop(0, steps, step, 0)

    def last(n, carry):
        slot = look(n, [i for i, _ in FINISH_LAST]) + 2 * source(look(n, [j for _, j in FINISH_LAST]))
        r_wait(slot)
        finish_math(slot, look(n, [state_of(i, j) for i, j in FINISH_LAST]), slot, slot)
        finish_send(slot)
        return carry

    lax.fori_loop(0, len(FINISH_LAST), last, 0)

    for dj, gg in peers:
        q_copy(dj, gg).wait_send()
        n_copy(dj, gg).wait_send()
    for i in range(2):
        z_copy(i).wait_send()
        x_copy(i).wait_send()
    for slot in range(2, 2 * ny):
        forward_copy(slot).wait_send()
    for p, (kind, j) in enumerate(ORDER):
        if kind != "Y":
            r_copy(p).wait_send()
    for slot in range(2 * ny):
        tile, yy = slot % 2, lax.rem(y + slot // 2, ny)
        if slot < 2:

            @pl.when(g == slot)
            def _():
                o_local(slot).wait()
                l_local(slot).wait()

            @pl.when(g != slot)
            def _():
                o_remote(slot, tile, yy).wait_send()
                l_remote(slot, tile, yy).wait_send()
        else:
            o_remote(slot, tile, yy).wait_send()
            l_remote(slot, tile, yy).wait_send()
    for dj, gg in peers:
        yy = row(dj)
        block = 2 * yy + gg
        pltpu.make_async_remote_copy(
            src_ref=o_stage.at[0], dst_ref=o_out.at[:, heads_of(gg, yy), :],
            send_sem=o_send.at[0], recv_sem=o_recv.at[block], device_id=other, device_id_type=MESH,
        ).wait_recv()
        pltpu.make_async_remote_copy(
            src_ref=lse_stage.at[0], dst_ref=lse_out.at[block],
            send_sem=l_send.at[0], recv_sem=l_recv.at[block], device_id=other, device_id_type=MESH,
        ).wait_recv()


def last_kernel(tok, grp, o_in, lse_in, o_out, lse_out, sem):
    copy = pltpu.make_async_copy(o_in, o_out, sem)
    copy.start()
    blocks, _, rows = lse_in.shape
    token = lax.broadcasted_iota(jnp.int32, (tok, rows), 0)
    owner = lax.div(lax.broadcasted_iota(jnp.int32, (tok, rows), 1), grp)
    head = lax.rem(lax.broadcasted_iota(jnp.int32, (rows, blocks * grp), 0), grp)
    column = lax.broadcasted_iota(jnp.int32, (rows, blocks * grp), 1)
    out = None
    for block in range(blocks):
        spread = jnp.where(token == owner, lse_in[block, 0:1, :], 0.0)
        place = (column == head + block * grp).astype(jnp.bfloat16)
        hi = spread.astype(jnp.bfloat16)
        rest = spread - hi.astype(jnp.float32)
        mid = rest.astype(jnp.bfloat16)
        low = (rest - mid.astype(jnp.float32)).astype(jnp.bfloat16)
        piece = dot(hi, place, 1, 0) + (dot(mid, place, 1, 0) + dot(low, place, 1, 0))
        out = piece if out is None else out + piece
    lse_out[...] = out
    copy.wait()


def body(queries, cache_keys, cache_values, new_keys, new_values, counts):
    nb, ny = lax.axis_size("blk"), lax.axis_size("kv")
    tok, nq, hd = queries.shape
    cap, kvl, _ = cache_keys.shape
    nh = new_keys.shape[1]
    grp = nq // nh
    rows = tok * grp
    bf16, f32 = jnp.bfloat16, jnp.float32
    vmem, dma = pltpu.VMEM, pltpu.SemaphoreType.DMA
    any_space = pl.BlockSpec(memory_space=pl.ANY)
    steps, own = len(ORDER), 2 * ny
    attended, lse = pl.pallas_call(
        functools.partial(kernel, nb, ny),
        out_shape=(
            jax.ShapeDtypeStruct((tok, nq, hd), bf16),
            jax.ShapeDtypeStruct((own, 8, rows), f32),
        ),
        in_specs=[pl.BlockSpec(memory_space=pltpu.SMEM)] + [any_space] * 5,
        out_specs=(any_space, any_space),
        scratch_shapes=[
            vmem((cap * kvl, hd), bf16), vmem((cap * kvl, hd), bf16), vmem((cap * kvl + 16, hd), f32),
            vmem((2, cap, hd), bf16), vmem((2, hd + EXT, cap), bf16),
            vmem((cap, hd), bf16), vmem((hd + EXT, cap), bf16),
            vmem((2 * own, tok, grp, hd), bf16),
            vmem((2, tok * nh, hd), bf16), vmem((own, 2, tok, hd), bf16), vmem((own, 2, tok, hd), bf16),
            vmem((cap, rows), f32), vmem((cap, rows), f32), vmem((8, rows), f32), vmem((8, rows), f32),
            vmem((cap, rows // 2), bf16), vmem((cap, rows // 2), bf16),
            vmem((hd, rows), f32), vmem((hd, rows), f32), vmem((2, cap // KC, 8, rows // 2), f32),
            vmem((2 * steps, hd + EXT, rows), bf16), vmem((own + 1, hd + EXT, rows), bf16),
            vmem((own + 1, tok, grp, hd), bf16), vmem((own + 1, 8, rows), f32),
            dma((4,)), dma((own,)), dma((2 * own,)), dma((2,)), dma((own,)), dma((own,)), dma((own,)),
            dma((2,)), dma((2,)), dma((own,)), dma((own,)), dma((own,)), dma((own,)), dma((own,)), dma((own,)),
        ],
        compiler_params=pltpu.CompilerParams(
            collective_id=0, has_side_effects=True, vmem_limit_bytes=56 * 2**20
        ),
    )(
        counts, queries, cache_keys.reshape(cap * kvl, hd), cache_values.reshape(cap * kvl, hd),
        new_keys.reshape(tok * nh, hd), new_values.reshape(tok * nh, hd),
    )
    return pl.pallas_call(
        functools.partial(last_kernel, tok, grp),
        out_shape=(jax.ShapeDtypeStruct((tok, nq, hd), bf16), jax.ShapeDtypeStruct((tok, nq), f32)),
        in_specs=[pl.BlockSpec(memory_space=vmem)] * 2,
        out_specs=(any_space, pl.BlockSpec(memory_space=vmem)),
        scratch_shapes=[dma],
    )(attended, lse)


def solution(mesh):
    in_specs = (
        P(("blk", "kv"), None, None),
        P("blk", "kv", None),
        P("blk", "kv", None),
        P(("blk", "kv"), None, None),
        P(("blk", "kv"), None, None),
        P("blk"),
    )
    out_specs = (P(("blk", "kv"), None, None), P(("blk", "kv"), None))
    return jax.shard_map(body, mesh=mesh, in_specs=in_specs, out_specs=out_specs, check_vma=False)
```

```python
import functools
import math

import jax
import jax.numpy as jnp
from jax import lax
from jax.experimental import pallas as pl
from jax.experimental.pallas import tpu as pltpu
from jax.sharding import PartitionSpec as P

MESH = pl.DeviceIdType.MESH
LOG2E = math.log2(math.e)
NEG = -1e30
KC = 256
BETWEEN = 4
EXT = 16

ORDER = (
    ("Y", 0), ("X", 0), ("Y", 1), ("Z", 0), ("X", 1), ("Z", 1),
    ("X", 2), ("Z", 2), ("Y", 2), ("X", 3), ("Z", 3), ("Y", 3),
)
FINISH = {4: (1, 0), 6: (0, 0), 7: (1, 1), 8: (0, 1), 9: (1, 2), 10: (0, 2)}
FINISH_LAST = ((1, 3), (0, 3))
FORWARD = {0: (1, 1), 1: (1, 0), 3: (2, 1), 4: (2, 0), 5: (3, 1), 6: (3, 0)}


def look(position, values):
    result = jnp.int32(values[-1])
    for i in reversed(range(len(values) - 1)):
        result = jnp.where(position == i, jnp.int32(values[i]), result)
    return result


def dot(a, b, ca, cb):
    return lax.dot_general(a, b, (((ca,), (cb,)), ((), ())), preferred_element_type=jnp.float32)


def pack_log(value):
    hi = value.astype(jnp.bfloat16).astype(jnp.float32)
    mid = (value - hi).astype(jnp.bfloat16).astype(jnp.float32)
    low = value - hi - mid
    row = lax.broadcasted_iota(jnp.int32, (EXT, value.shape[1]), 0)
    packed = jnp.where(row == 0, hi, jnp.where(row == 1, mid, jnp.where(row == 2, low, 0.0)))
    return packed.astype(jnp.bfloat16)


def unpack_log(rows):
    wide = rows.astype(jnp.float32)
    return wide[0:1] + wide[1:2] + wide[2:3]


def kernel(
    nb, ny,
    counts, q_in, ck_in, cv_in, nk_in, nv_in,
    o_out, lse_out,
    raw_k, raw_v, wide, k_buf, v_buf, k_send, v_send, qall, new_raw, new_send, new_buf,
    s0, s1, m0, m1, p0, p1, acc_a, acc_b, dead, res, part_in, o_stage, lse_stage,
    load_sem, q_send, q_recv, z_send, f_send, n_send, n_recv, x_send, x_recv,
    r_send, r_recv, o_send, o_recv, l_send, l_recv,
):
    cap = k_buf.shape[1]
    tok, grp, hd = qall.shape[1:]
    rows = tok * grp
    half = rows // 2
    scale = LOG2E / math.sqrt(hd)

    b = lax.axis_index("blk")
    y = lax.axis_index("kv")
    g = lax.rem(b, 2)
    chip0 = b - g
    prev0 = lax.rem(chip0 + nb - 2, nb)
    next0 = lax.rem(chip0 + 2, nb)
    other = (chip0 + 1 - g, y)

    peers = [(0, 1 - g)] + [(dj, gg) for dj in range(1, ny) for gg in range(2)]

    def row(dj):
        return lax.rem(y + dj, ny)

    def source(j):
        return lax.rem(ny + (1 - 2 * g) * j, ny)

    load_k = pltpu.make_async_copy(ck_in, raw_k, load_sem.at[0])
    load_v = pltpu.make_async_copy(cv_in, raw_v, load_sem.at[1])
    load_nk = pltpu.make_async_copy(nk_in, new_raw.at[0], load_sem.at[2])
    load_nv = pltpu.make_async_copy(nv_in, new_raw.at[1], load_sem.at[3])
    load_k.start()
    load_nk.start()
    load_nv.start()
    load_v.start()

    def heads_of(gg, yy):
        return pl.ds(pl.multiple_of((2 * yy + gg) * grp, grp), grp)

    load_q = pltpu.make_async_copy(q_in.at[:, heads_of(g, y), :], qall.at[g], q_recv.at[g])
    load_q.start()

    def q_copy(dj, gg):
        slot = ((ny - dj) % ny) * 2 + g
        return pltpu.make_async_remote_copy(
            src_ref=q_in.at[:, heads_of(gg, row(dj)), :], dst_ref=qall.at[slot],
            send_sem=q_send.at[2 * dj + gg], recv_sem=q_recv.at[slot],
            device_id=(chip0 + gg, row(dj)), device_id_type=MESH,
        )

    def z_copy(gg):
        slot = 2 * ny + g
        return pltpu.make_async_remote_copy(
            src_ref=q_in.at[:, heads_of(gg, y), :], dst_ref=qall.at[slot],
            send_sem=z_send.at[gg], recv_sem=q_recv.at[slot],
            device_id=(prev0 + gg, y), device_id_type=MESH,
        )

    def forward_copy(slot):
        return pltpu.make_async_remote_copy(
            src_ref=qall.at[slot], dst_ref=qall.at[2 * ny + slot],
            send_sem=f_send.at[slot], recv_sem=q_recv.at[2 * ny + slot],
            device_id=(prev0 + g, y), device_id_type=MESH,
        )

    def q_wait(slot):
        pltpu.make_async_remote_copy(
            src_ref=qall.at[slot], dst_ref=qall.at[slot],
            send_sem=f_send.at[0], recv_sem=q_recv.at[slot],
            device_id=other, device_id_type=MESH,
        ).wait_recv()

    barrier = pltpu.get_barrier_semaphore()
    for dj, gg in peers:
        pl.semaphore_signal(barrier, inc=1, device_id=(chip0 + gg, row(dj)), device_id_type=MESH)
    for base in (prev0, next0):
        for i in range(2):
            pl.semaphore_signal(barrier, inc=1, device_id=(base + i, y), device_id_type=MESH)

    nh = new_raw.shape[1] // tok

    def n_copy(dj, gg):
        slot = ((ny - dj) % ny) * 2 + g
        n = 2 * dj + gg
        return pltpu.make_async_remote_copy(
            src_ref=new_send.at[n], dst_ref=new_buf.at[slot],
            send_sem=n_send.at[n], recv_sem=n_recv.at[slot],
            device_id=(chip0 + gg, row(dj)), device_id_type=MESH,
        )

    load_nk.wait()
    load_nv.wait()
    for kind in range(2):
        wide[kind * tok * nh : (kind + 1) * tok * nh, :] = new_raw[kind].astype(jnp.float32)
    for kind in range(2):
        for dj in range(ny):
            for gg in range(2):
                head = 2 * row(dj) + gg
                x = wide[pl.ds(kind * tok * nh + head, tok, stride=nh), :].astype(jnp.bfloat16)
                new_send[2 * dj + gg, kind] = x
        new_buf[g, kind] = new_send[g, kind]

    live = counts[0]

    def x_copy(n):
        src, dst = ((k_send, k_buf), (v_send, v_buf))[n]
        return pltpu.make_async_remote_copy(
            src_ref=src, dst_ref=dst.at[g], send_sem=x_send.at[n], recv_sem=x_recv.at[n],
            device_id=other, device_id_type=MESH,
        )

    load_k.wait()
    top_rows = raw_k[0:16, :].astype(jnp.float32)
    first_keys = [jnp.where(head == 0, top_rows[0:1], top_rows[1:2]) for head in (1 - g, g)]

    def split_keys(c, carry):
        at = pl.multiple_of(c * KC, KC)
        wide[pl.ds(2 * at, 2 * KC), :] = raw_k[pl.ds(2 * at, 2 * KC), :].astype(jnp.float32)
        index = lax.broadcasted_iota(jnp.int32, (KC, hd), 0) + at
        for n, head in enumerate((1 - g, g)):
            x = wide[pl.ds(2 * at + head, KC, stride=2), :]
            x = jnp.where(index < live, x, first_keys[n]).astype(jnp.bfloat16)
            if n == 0:
                k_send[pl.ds(at, KC), :] = x
            else:
                k_buf[g, pl.ds(at, KC), :] = x
        return carry

    lax.fori_loop(0, cap // KC, split_keys, 0)
    pl.semaphore_wait(barrier, len(peers) + 4)
    x_copy(0).start()
    q_copy(0, 1 - g).start()

    @pl.when(g == 1)
    def _():
        z_copy(0).start()
        z_copy(1).start()

    for dj, gg in peers:
        n_copy(dj, gg).start()

    q_copy(ny - 1, 0).start()
    q_copy(1, 1).start()

    load_v.wait()

    def split_values(c, carry):
        at = pl.multiple_of(c * KC, KC)
        wide[pl.ds(2 * at, 2 * KC), :] = raw_v[pl.ds(2 * at, 2 * KC), :].astype(jnp.float32)
        column = lax.broadcasted_iota(jnp.int32, (hd, KC), 1) + at
        mark_row = lax.broadcasted_iota(jnp.int32, (EXT, KC), 0)
        mark_column = lax.broadcasted_iota(jnp.int32, (EXT, KC), 1) + at
        marks = jnp.where((mark_row == 0) & (mark_column < live), 1.0, 0.0).astype(jnp.bfloat16)
        for n, head in enumerate((1 - g, g)):
            x = wide[pl.ds(2 * at + head, KC, stride=2), :]
            x = jnp.where(column < live, x.T, 0.0).astype(jnp.bfloat16)
            if n == 0:
                v_send[0:hd, pl.ds(at, KC)] = x
                v_send[hd : hd + EXT, pl.ds(at, KC)] = marks
            else:
                v_buf[g, 0:hd, pl.ds(at, KC)] = x
                v_buf[g, hd : hd + EXT, pl.ds(at, KC)] = marks
        return carry

    lax.fori_loop(0, cap // KC, split_values, 0)

    x_copy(1).start()

    def scores(qa, t, seg, kk):
        qq = qall[qa, t * (tok // 2) : (t + 1) * (tok // 2)].reshape(half, hd)
        return dot(k_buf[seg, kk, :], qq, 1, 1)

    def fold(chunk):
        return jnp.max(chunk.reshape(KC // 8, 8, half), axis=0)

    def first(qa, seg, s_ref, m_ref):
        for t in range(2):
            cols = slice(t * half, (t + 1) * half)
            top = None
            for c in range(cap // KC):
                kk = slice(c * KC, (c + 1) * KC)
                s = scores(qa, t, seg, kk)
                s_ref[kk, cols] = s
                top = fold(s) if top is None else jnp.maximum(top, fold(s))
            m_ref[:, cols] = jnp.broadcast_to(jnp.max(top, axis=0, keepdims=True), (8, half))

    def tile(t, qa, seg, s_new, m_new, s_old, m_old, seg_old, between):
        cols = slice(t * half, (t + 1) * half)
        p_ref = (p0, p1)[t]
        old = m_old[0:1, cols] * scale
        top = total = None
        for c in range(cap // KC):
            if c == BETWEEN:
                between()
            kk = slice(c * KC, (c + 1) * KC)
            s = scores(qa, t, seg, kk)
            s_new[kk, cols] = s
            top = fold(s) if top is None else jnp.maximum(top, fold(s))
            p = jnp.exp2(s_old[kk, cols] * scale - old)
            p_ref[kk, :] = p.astype(jnp.bfloat16)
            if c == 0:
                weight_0 = p[0:1, :]
            part = jnp.sum(p.reshape(KC // 8, 8, half), axis=0) - dead[seg_old, c] * weight_0
            total = part if total is None else total + part
        m_new[:, cols] = jnp.broadcast_to(jnp.max(top, axis=0, keepdims=True), (8, half))
        return jnp.sum(total, axis=0, keepdims=True)

    def mix_half(t, seg, acc):
        acc[:, t * half : (t + 1) * half] = dot(v_buf[seg, 0:hd], (p0, p1)[t][...], 1, 0)

    def log2(x):
        return jnp.log(x) * LOG2E

    steps = len(ORDER)
    kinds = [k for k, _ in ORDER]
    sources = [j for _, j in ORDER]
    own = 2 * ny
    base_a = [{"X": 0, "Y": 1, "Z": own}[k] for k in kinds]
    base_b = [{"X": own + 1, "Y": 1, "Z": own}[k] for k in kinds]
    part_tile = [int(k == "X") for k in kinds]

    def qa_at(p):
        return look(p, base_a) + 2 * source(look(p, sources))

    def qb_at(p):
        return look(p, base_b) + 2 * source(look(p, sources))

    def seg_at(p):
        return g * look(p, [int(k != "X") for k in kinds])

    at_steps = [FINISH.get(p, (0, 0)) for p in range(steps)]

    def r_copy(p):
        slot = look(p, part_tile) + 2 * source(look(p, sources))
        return pltpu.make_async_remote_copy(
            src_ref=res.at[2 * p + 1], dst_ref=part_in.at[slot],
            send_sem=r_send.at[slot], recv_sem=r_recv.at[slot],
            device_id=(next0 + g, y), device_id_type=MESH,
        )

    def r_wait(slot):
        pltpu.make_async_remote_copy(
            src_ref=part_in.at[slot], dst_ref=part_in.at[slot],
            send_sem=r_send.at[slot], recv_sem=r_recv.at[slot],
            device_id=other, device_id_type=MESH,
        ).wait_recv()

    own_heads = heads_of(g, y)
    own_block = 2 * y + g

    def o_remote(slot, tile, yy):
        return pltpu.make_async_remote_copy(
            src_ref=o_stage.at[slot], dst_ref=o_out.at[:, own_heads, :],
            send_sem=o_send.at[slot], recv_sem=o_recv.at[own_block],
            device_id=(chip0 + tile, yy), device_id_type=MESH,
        )

    def l_remote(slot, tile, yy):
        return pltpu.make_async_remote_copy(
            src_ref=lse_stage.at[slot], dst_ref=lse_out.at[own_block],
            send_sem=l_send.at[slot], recv_sem=l_recv.at[own_block],
            device_id=(chip0 + tile, yy), device_id_type=MESH,
        )

    def o_local(slot):
        return pltpu.make_async_copy(o_stage.at[slot], o_out.at[:, own_heads, :], o_send.at[slot])

    def l_local(slot):
        return pltpu.make_async_copy(lse_stage.at[slot], lse_out.at[own_block], l_send.at[slot])

    def slot_of(tile, j):
        return 2 * source(j) + tile

    def finish_math(slot, src, part, stage):
        tile = lax.rem(slot, 2)
        yy = lax.rem(y + lax.div(slot, 2), ny)
        queries = qall[slot].reshape(rows, hd)
        keys = jnp.concatenate([new_buf[2 * j + tile, 0] for j in range(ny)], axis=0)
        vals = jnp.concatenate([new_buf[2 * j + tile, 1] for j in range(ny)], axis=0)
        s = dot(keys, queries, 1, 1)
        key_row = lax.broadcasted_iota(jnp.int32, s.shape, 0)
        key_pos = lax.rem(lax.div(key_row, tok) + y, ny) * tok + lax.rem(key_row, tok)
        token = lax.div(lax.broadcasted_iota(jnp.int32, s.shape, 1), grp) + yy * tok
        s = jnp.where(key_pos <= token, s, NEG)
        top = jnp.max(s, axis=0, keepdims=True)
        p = jnp.exp2((s - top) * scale)
        total = jnp.sum(p, axis=0, keepdims=True)
        mix = dot(vals, p.astype(jnp.bfloat16), 0, 0)
        e0 = top * scale
        e1 = unpack_log(res[src, hd : hd + EXT, :])
        e2 = unpack_log(part_in[part, hd : hd + EXT, :])
        high = jnp.maximum(e0, jnp.maximum(e1, e2))
        w0 = jnp.exp2(e0 - high)
        w1 = jnp.exp2(e1 - high)
        w2 = jnp.exp2(e2 - high)
        whole = w0 * total + w1 + w2
        inv = 1.0 / whole
        out = mix * (w0 * inv)
        out += res[src, 0:hd, :].astype(jnp.float32) * (w1 * inv)
        out += part_in[part, 0:hd, :].astype(jnp.float32) * (w2 * inv)
        o_stage[stage] = out.T.astype(jnp.bfloat16).reshape(tok, grp, hd)
        lse_stage[stage] = jnp.broadcast_to((high + log2(whole)) * (1.0 / LOG2E), (8, rows))

    def finish_send(slot):
        tile = lax.rem(slot, 2)
        yy = lax.rem(y + lax.div(slot, 2), ny)
        mine = slot == g

        @pl.when(mine)
        def _():
            o_local(slot).start()
            l_local(slot).start()

        @pl.when(jnp.logical_not(mine))
        def _():
            o_remote(slot, tile, yy).start()
            l_remote(slot, tile, yy).start()

    def state_of(tile, j):
        return 2 * ORDER.index(("X", j)) if tile == 0 else 2 * ORDER.index(("Y", j)) + 1

    load_q.wait()
    q_wait(1 - g)
    first(qa_at(0), seg_at(0), s0, m0)

    @pl.when(g == 0)
    def _():
        z_copy(0).start()
        z_copy(1).start()

    for dj in range(2, ny - 1):
        for gg in range(2):
            q_copy(dj, gg).start()
    for dj, gg in peers:
        slot = 2 * dj + gg
        pltpu.make_async_remote_copy(
            src_ref=new_buf.at[slot], dst_ref=new_buf.at[slot],
            send_sem=n_send.at[0], recv_sem=n_recv.at[slot], device_id=other, device_id_type=MESH,
        ).wait_recv()
    x_copy(0).wait_recv()
    x_copy(1).wait_recv()
    for seg in range(2):
        for c in range(cap // KC):
            marks = v_buf[seg, hd : hd + EXT, c * KC : (c + 1) * KC].astype(jnp.float32)
            rows_live = jnp.sum(jnp.sum(marks, axis=0, keepdims=True), axis=1, keepdims=True)
            dead[seg, c] = jnp.broadcast_to((KC - rows_live) * 0.125, (8, half))

    def block_at(p):
        return look(p, [i for i, _ in at_steps]) + 2 * source(look(p, [j for _, j in at_steps]))

    def step(p, carry):
        later = lax.rem(p + 1, steps)
        kind_x = look(p, [int(k == "X") for k in kinds])
        ends_block = look(p, [int(q in FINISH) for q in range(steps)]) == 1
        done = block_at(p)
        done_state = look(p, [state_of(i, j) for i, j in at_steps])

        spare = jnp.where(ends_block, done, own)
        top_a = m0[0:1, :] * scale
        qb, qa = qb_at(p), qa_at(later)
        seg_a, seg_later = seg_at(p), seg_at(later)
        seg_b = 1 - seg_a
        a0 = tile(0, qb, seg_b, s1, m1, s0, m0, seg_a, lambda: finish_math(done, done_state, spare, spare))
        a1 = tile(1, qb, seg_b, s1, m1, s0, m0, seg_a, lambda: mix_half(0, seg_a, acc_a))
        top_b = m1[0:1, :] * scale
        b0 = tile(0, qa, seg_later, s0, m0, s1, m1, seg_b, lambda: mix_half(1, seg_a, acc_a))
        b1 = tile(1, qa, seg_later, s0, m0, s1, m1, seg_b, lambda: mix_half(0, seg_b, acc_b))
        mix_half(1, seg_b, acc_b)
        total_a = jnp.concatenate([a0, a1], axis=1)
        ea = top_a + log2(total_a)
        res[2 * p, 0:hd, :] = (acc_a[...] * (1.0 / total_a)).astype(jnp.bfloat16)
        res[2 * p, hd : hd + EXT, :] = pack_log(ea)
        total_b = jnp.concatenate([b0, b1], axis=1)
        eb = top_b + log2(total_b)
        ea = ea + jnp.where(kind_x == 1, NEG, 0.0)
        high = jnp.maximum(ea, eb)
        wa = jnp.exp2(ea - high)
        wb = jnp.exp2(eb - high)
        whole = wa + wb
        merged = acc_a[...] * (wa / (whole * total_a)) + acc_b[...] * (wb / (whole * total_b))
        res[2 * p + 1, 0:hd, :] = merged.astype(jnp.bfloat16)
        res[2 * p + 1, hd : hd + EXT, :] = pack_log(high + log2(whole))

        @pl.when(look(p, [int(k != "Y") for k in kinds]) == 1)
        def _():
            r_copy(p).start()

        @pl.when(ends_block)
        def _():
            finish_send(done)

        @pl.when(look(p, [int(at in FORWARD) for at in range(steps)]) == 1)
        def _():
            entries = [FORWARD.get(at, (0, 0)) for at in range(steps)]
            slot = 2 * source(look(p, [j for j, _ in entries])) + look(p, [i for _, i in entries])
            q_wait(slot)
            forward_copy(slot).start()

        @pl.when(p == 2)
        def _():
            q_copy(ny - 1, 1).start()
            q_copy(1, 0).start()

        @pl.when(look(p, [int(k == "X") for k in kinds[1:]] + [0]) == 1)
        def _():
            q_wait(qb_at(p + 1))

        @pl.when(look(p, [int(k == "Z") for k in kinds[2:]] + [0, 0]) == 1)
        def _():
            q_wait(qa_at(p + 2))

        @pl.when(look(p, [int(q + 1 in FINISH) for q in range(steps)]) == 1)
        def _():
            r_wait(block_at(p + 1))

        return carry

    lax.fori_loop(0, steps, step, 0)

    def last(n, carry):
        slot = look(n, [i for i, _ in FINISH_LAST]) + 2 * source(look(n, [j for _, j in FINISH_LAST]))
        r_wait(slot)
        finish_math(slot, look(n, [state_of(i, j) for i, j in FINISH_LAST]), slot, slot)
        finish_send(slot)
        return carry

    lax.fori_loop(0, len(FINISH_LAST), last, 0)

    for dj, gg in peers:
        q_copy(dj, gg).wait_send()
        n_copy(dj, gg).wait_send()
    for i in range(2):
        z_copy(i).wait_send()
        x_copy(i).wait_send()
    for slot in range(2, 2 * ny):
        forward_copy(slot).wait_send()
    for p, (kind, j) in enumerate(ORDER):
        if kind != "Y":
            r_copy(p).wait_send()
    for slot in range(2 * ny):
        tile, yy = slot % 2, lax.rem(y + slot // 2, ny)
        if slot < 2:

            @pl.when(g == slot)
            def _():
                o_local(slot).wait()
                l_local(slot).wait()

            @pl.when(g != slot)
            def _():
                o_remote(slot, tile, yy).wait_send()
                l_remote(slot, tile, yy).wait_send()
        else:
            o_remote(slot, tile, yy).wait_send()
            l_remote(slot, tile, yy).wait_send()
    for dj, gg in peers:
        yy = row(dj)
        block = 2 * yy + gg
        pltpu.make_async_remote_copy(
            src_ref=o_stage.at[0], dst_ref=o_out.at[:, heads_of(gg, yy), :],
            send_sem=o_send.at[0], recv_sem=o_recv.at[block], device_id=other, device_id_type=MESH,
        ).wait_recv()
        pltpu.make_async_remote_copy(
            src_ref=lse_stage.at[0], dst_ref=lse_out.at[block],
            send_sem=l_send.at[0], recv_sem=l_recv.at[block], device_id=other, device_id_type=MESH,
        ).wait_recv()


def last_kernel(tok, grp, o_in, lse_in, o_out, lse_out, sem):
    copy = pltpu.make_async_copy(o_in, o_out, sem)
    copy.start()
    blocks, _, rows = lse_in.shape
    token = lax.broadcasted_iota(jnp.int32, (tok, rows), 0)
    owner = lax.div(lax.broadcasted_iota(jnp.int32, (tok, rows), 1), grp)
    head = lax.rem(lax.broadcasted_iota(jnp.int32, (rows, blocks * grp), 0), grp)
    column = lax.broadcasted_iota(jnp.int32, (rows, blocks * grp), 1)
    out = None
    for block in range(blocks):
        spread = jnp.where(token == owner, lse_in[block, 0:1, :], 0.0)
        place = (column == head + block * grp).astype(jnp.bfloat16)
        hi = spread.astype(jnp.bfloat16)
        rest = spread - hi.astype(jnp.float32)
        mid = rest.astype(jnp.bfloat16)
        low = (rest - mid.astype(jnp.float32)).astype(jnp.bfloat16)
        piece = dot(hi, place, 1, 0) + (dot(mid, place, 1, 0) + dot(low, place, 1, 0))
        out = piece if out is None else out + piece
    lse_out[...] = out
    copy.wait()


def body(queries, cache_keys, cache_values, new_keys, new_values, counts):
    nb, ny = lax.axis_size("blk"), lax.axis_size("kv")
    tok, nq, hd = queries.shape
    cap, kvl, _ = cache_keys.shape
    nh = new_keys.shape[1]
    grp = nq // nh
    rows = tok * grp
    bf16, f32 = jnp.bfloat16, jnp.float32
    vmem, dma = pltpu.VMEM, pltpu.SemaphoreType.DMA
    any_space = pl.BlockSpec(memory_space=pl.ANY)
    steps, own = len(ORDER), 2 * ny
    attended, lse = pl.pallas_call(
        functools.partial(kernel, nb, ny),
        out_shape=(
            jax.ShapeDtypeStruct((tok, nq, hd), bf16),
            jax.ShapeDtypeStruct((own, 8, rows), f32),
        ),
        in_specs=[pl.BlockSpec(memory_space=pltpu.SMEM)] + [any_space] * 5,
        out_specs=(any_space, any_space),
        scratch_shapes=[
            vmem((cap * kvl, hd), bf16), vmem((cap * kvl, hd), bf16), vmem((cap * kvl + 16, hd), f32),
            vmem((2, cap, hd), bf16), vmem((2, hd + EXT, cap), bf16),
            vmem((cap, hd), bf16), vmem((hd + EXT, cap), bf16),
            vmem((2 * own, tok, grp, hd), bf16),
            vmem((2, tok * nh, hd), bf16), vmem((own, 2, tok, hd), bf16), vmem((own, 2, tok, hd), bf16),
            vmem((cap, rows), f32), vmem((cap, rows), f32), vmem((8, rows), f32), vmem((8, rows), f32),
            vmem((cap, rows // 2), bf16), vmem((cap, rows // 2), bf16),
            vmem((hd, rows), f32), vmem((hd, rows), f32), vmem((2, cap // KC, 8, rows // 2), f32),
            vmem((2 * steps, hd + EXT, rows), bf16), vmem((own + 1, hd + EXT, rows), bf16),
            vmem((own + 1, tok, grp, hd), bf16), vmem((own + 1, 8, rows), f32),
            dma((4,)), dma((own,)), dma((2 * own,)), dma((2,)), dma((own,)), dma((own,)), dma((own,)),
            dma((2,)), dma((2,)), dma((own,)), dma((own,)), dma((own,)), dma((own,)), dma((own,)), dma((own,)),
        ],
        compiler_params=pltpu.CompilerParams(
            collective_id=0, has_side_effects=True, vmem_limit_bytes=56 * 2**20
        ),
    )(
        counts, queries, cache_keys.reshape(cap * kvl, hd), cache_values.reshape(cap * kvl, hd),
        new_keys.reshape(tok * nh, hd), new_values.reshape(tok * nh, hd),
    )
    return pl.pallas_call(
        functools.partial(last_kernel, tok, grp),
        out_shape=(jax.ShapeDtypeStruct((tok, nq, hd), bf16), jax.ShapeDtypeStruct((tok, nq), f32)),
        in_specs=[pl.BlockSpec(memory_space=vmem)] * 2,
        out_specs=(any_space, pl.BlockSpec(memory_space=vmem)),
        scratch_shapes=[dma],
    )(attended, lse)


def solution(mesh):
    in_specs = (
        P(("blk", "kv"), None, None),
        P("blk", "kv", None),
        P("blk", "kv", None),
        P(("blk", "kv"), None, None),
        P(("blk", "kv"), None, None),
        P("blk"),
    )
    out_specs = (P(("blk", "kv"), None, None), P(("blk", "kv"), None))
    return jax.shard_map(body, mesh=mesh, in_specs=in_specs, out_specs=out_specs, check_vma=False)
```
